256 devices in a mesh: cache: 32 (over x, y, core), mp: 8 (over z).
Axes of the slice: x: 4, y: 4, z: 8, core: 2. Of those that a mesh axis runs over, the one named last changes fastest.
Arguments:
- cand_rows: bfloat16 [32768, 1024], P('cache', 'mp'), may hold values from -6 to 6
- w_in: bfloat16 [1024, 8, 256], P(None, 'mp'), may hold values from -0.1875 to 0.1875
- w_out: bfloat16 [8, 128, 1024], P('mp'), may hold values from -0.25 to 0.25
- kv_pool: bfloat16 [2, 4096, 128, 1024], P(None, 'cache', None, 'mp'), may hold values from -6 to 6
- send_list: int32 [32, 128], P('cache'), may hold values from 0 to 127, each once within a row
- block_live: int32 [32, 128], P('cache'), may hold values from 0 to 1, as said below
- cand_count: int32 [32], P('cache'), may hold values from 128 to 1024, as said below
Outputs:
- ranked: bfloat16 [32768, 1024], P('cache', 'mp')
The draws below stay inside these ranges and needn't reach their ends.
Inputs may be any that keep to these rules, and one draw needn't show every extreme that they name: `block_live`: among the 4 slots that one owner keeps for one ranker at most 2 are live; some ranker has exactly 2 live slots from every owner. `cand_count`: some ranker has exactly 1024 live rows. `send_list`: each row is a permutation of the owner's 128 pool blocks.
All inputs are finite; a program needn't handle non-finite values.
Results may differ from the reference program's by a relative error of at most 0.015.
Values may be sent and summed in bfloat16 or wider, within the bound.
No kernel may reach another device: no remote copies, remote signals or barrier semaphores. Data moves between devices by JAX's collectives and lax.ppermute only.
A program may use at most 128 MiB of HBM per device.

```python
import math
import jax
import jax.numpy as jnp
from jax import lax

D = 1024
H = 8
HS = 128
BLK = 128
SLOTS = 4
LIVE = 2
TOK = 1024
POOL = 128
TOKENS = 32768
N_CACHE = 32
N_MP = 8


def draw_block_live(key, part):
    key = jax.random.fold_in(key, 11)
    first, second, third = jax.random.split(key, 3)
    ranks = POOL // SLOTS
    count = jax.random.randint(first, (ranks, ranks), 1, LIVE + 1)
    full_rank = jax.random.randint(second, (), 0, ranks)
    count = jnp.where(jnp.arange(ranks)[None, :] == full_rank, LIVE, count)
    scores = jax.random.randint(third, (ranks, ranks, SLOTS), 0, 1 << 20) * SLOTS + jnp.arange(SLOTS)[None, None, :]
    order = jnp.argsort(jnp.argsort(scores, axis=-1), axis=-1)
    live = (order < count[..., None]).astype(jnp.int32)
    return live.reshape(ranks, POOL)


def draw_cand_count(key, part):
    key = jax.random.fold_in(key, 23)
    first, second = jax.random.split(key)
    ranks = POOL // SLOTS
    counts = jax.random.randint(first, (ranks,), TOK // 8, TOK // 2 + 1)
    full_rank = jax.random.randint(second, (), 0, ranks)
    return jnp.where(jnp.arange(ranks) == full_rank, TOK, counts).astype(jnp.int32)


def raised(values, rng, source, target, blocks, factor):
    def block_of(dim):
        return (jnp.arange(values.shape[dim]) // (values.shape[dim] // blocks)).reshape((-1,) + (1,) * (values.ndim - 1 - dim))

    first = jax.random.permutation(rng, blocks)[block_of(target)]
    second = (block_of(target) + blocks // 2) % blocks
    return jnp.where((block_of(source) == first) | (block_of(source) == second), factor * values, values)


def shard_levels(own_key, dims, cuts, least, largest):
    def one(axis_at, blocks):
        draws = jax.random.uniform(jax.random.fold_in(jax.random.fold_in(own_key, 6), axis_at), (blocks,), jnp.float32, least / len(cuts), largest / len(cuts))
        return jnp.repeat(jnp.exp(draws), dims[axis_at] // blocks).reshape((-1,) + (1,) * (len(dims) - axis_at - 1))

    level = one(*cuts[0])
    for cut in cuts[1:]:
        level = level * one(*cut)
    return level


def normal_values(rng, dims, scale, limit, cuts=(), kind=jnp.bfloat16):
    entries = scale * jax.random.normal(rng, dims, jnp.float32)
    if cuts:
        entries = entries * shard_levels(rng, dims, cuts, -0.22, 0.18)
    return jnp.clip(entries, -limit, limit).astype(kind)


def heavy_noise(stream_key, shape, width, bound, cuts, heavy, held_as=jnp.bfloat16):
    entries = width * jax.random.normal(stream_key, shape, jnp.float32)
    if cuts:
        entries = entries * shard_levels(stream_key, shape, cuts, -0.22, 0.18)
    return jnp.clip(raised(entries, jax.random.fold_in(stream_key, 3), *heavy), -bound, bound).astype(held_as)


def setup_inputs(seed: int = 0) -> dict:
    key_of = jax.random.split(jax.random.key(seed), 8)
    cand_rows = normal_values(key_of[0], (TOKENS, D), 1.0, 6.0, ((0, 32), (1, 8)))
    w_in = normal_values(key_of[1], (D, H, 2 * HS), D ** -0.5, 0.1875, ((1, 8),))
    w_out = heavy_noise(key_of[2], (H, HS, D), (H * HS) ** -0.5, 0.25, ((0, 8),), (0, 2, 8, 2.0))
    kv_pool = normal_values(key_of[3], (2, N_CACHE * POOL, BLK, H * HS), 1.0, 6.0, ((1, 32), (3, 8)))
    send_list = jax.vmap(lambda own: jax.random.permutation(own, POOL))(jax.random.split(key_of[4], N_CACHE)).reshape((N_CACHE, POOL)).astype(jnp.int32)
    block_live = draw_block_live(jax.random.fold_in(key_of[7], 71), 0)
    cand_count = draw_cand_count(jax.random.fold_in(key_of[7], 71), 0)
    return dict(cand_rows=cand_rows, w_in=w_in, w_out=w_out, kv_pool=kv_pool, send_list=send_list, block_live=block_live, cand_count=cand_count)


def rounded(value):
    return lax.optimization_barrier(value.astype(jnp.bfloat16)).astype(jnp.float32)

def reference(cand_rows, w_in, w_out, kv_pool, send_list, block_live, cand_count):
    keys_all = N_CACHE * SLOTS * BLK
    step_keys = math.gcd(keys_all, 4096)
    slot_ids = jnp.arange(SLOTS, dtype=jnp.int32)
    owners = jnp.arange(N_CACHE, dtype=jnp.int32)
    w_in32 = w_in.astype(jnp.float32)
    w_out_groups = w_out.astype(jnp.float32).reshape(N_MP, H * HS // N_MP, D)
    scale = HS ** (-0.5)

    def per_ranker(ranker):
        rows = lax.dynamic_slice_in_dim(cand_rows, (ranker * TOK).astype(jnp.int32), TOK, 0)
        proj = jnp.einsum('td,dhe->the', rows.astype(jnp.float32), w_in32)
        gate = jax.nn.silu(proj[..., :HS])
        query = rounded(jax.nn.silu(proj[..., HS:]))
        columns = ranker * SLOTS + slot_ids
        local = send_list[:, columns]
        live = block_live[:, columns]
        index = (owners[:, None] * POOL + local).reshape(-1).astype(jnp.int32)
        blocks = kv_pool[:, index] * live.reshape(-1)[None, :, None, None].astype(jnp.bfloat16)
        blocks = blocks.reshape(2, keys_all // step_keys, step_keys, H, HS)
        blocks = jnp.moveaxis(blocks, 1, 0)

        def accumulate(total, pair):
            keys = pair[0].astype(jnp.float32)
            values = pair[1].astype(jnp.float32)
            score = jnp.einsum('thd,khd->thk', query, keys) * scale
            weight = rounded(jax.nn.silu(score))
            return (total + jnp.einsum('thk,khd->thd', weight, values), None)
        attended, _ = lax.scan(accumulate, jnp.zeros((TOK, H, HS), jnp.float32), blocks)
        center = attended - lax.optimization_barrier(jnp.mean(attended, axis=-1, keepdims=True))
        variance = lax.optimization_barrier(jnp.mean(center * center, axis=-1, keepdims=True))
        gated = rounded(center / jnp.sqrt(variance + 1e-05) * gate)
        parts = jnp.einsum('tgc,gcd->gtd', gated.reshape(TOK, N_MP, H * HS // N_MP), w_out_groups)
        total = rows.astype(jnp.float32) + lax.optimization_barrier(jnp.sum(rounded(parts), axis=0))
        keep = (jnp.arange(TOK, dtype=jnp.int32) < cand_count[ranker])[:, None]
        return jnp.where(keep, total, jnp.float32(0.0)).astype(jnp.bfloat16)
    ranked = lax.map(per_ranker, jnp.arange(N_CACHE, dtype=jnp.int32))
    return ranked.reshape(N_CACHE * TOK, D)
```

```python
import jax
import jax.numpy as jnp
from jax import lax
from jax.experimental import pallas as pl
from jax.experimental.pallas import tpu as pltpu
from jax.sharding import PartitionSpec as P

BF16 = jnp.bfloat16
F32 = jnp.float32
VMEM = 16 * 1024 * 1024
LIVE = 2
PARTS = 2


def pack_live(send_list, block_live, kv_pool):
    pool = kv_pool.shape[1]
    tile = kv_pool.shape[2:]
    rankers = lax.axis_size("cache")
    slots = pool // rankers

    def body(send_hbm, live_hbm, pool_ref, out_ref, send_ref, live_ref, sem, list_sem):
        lists = [
            pltpu.make_async_copy(send_hbm, send_ref, list_sem.at[0]),
            pltpu.make_async_copy(live_hbm, live_ref, list_sem.at[1]),
        ]
        for copy in lists:
            copy.start()
        for copy in lists:
            copy.wait()

        def one(r, copies):
            seen = jnp.int32(0)
            blocks = [jnp.int32(0)] * LIVE
            for s in range(slots):
                live = live_ref[0, r * slots + s]
                for k in range(LIVE):
                    hit = jnp.logical_and(seen == k, live > 0)
                    blocks[k] = jnp.where(hit, send_ref[0, r * slots + s], blocks[k])
                seen = seen + live
            for k in range(LIVE):

                @pl.when(seen > k)
                def _():
                    pltpu.make_async_copy(
                        pool_ref.at[:, blocks[k]], out_ref.at[r, pl.ds(2 * k, 2)], sem
                    ).start()

                @pl.when(seen <= k)
                def _():
                    out_ref[r, pl.ds(2 * k, 2)] = jnp.zeros((2,) + tile, BF16)

            return copies + jnp.minimum(seen, LIVE)

        def done(_, carry):
            half = out_ref.at[0, pl.ds(0, 2)]
            pltpu.make_async_copy(half, half, sem).wait()
            return carry

        copies = lax.fori_loop(0, rankers, one, jnp.int32(0), unroll=4)
        lax.fori_loop(0, copies, done, 0)

    hbm = pl.BlockSpec(memory_space=pltpu.HBM)
    return pl.pallas_call(
        body,
        out_shape=jax.ShapeDtypeStruct((rankers, 2 * LIVE) + tile, BF16),
        in_specs=[hbm, hbm, hbm],
        out_specs=pl.BlockSpec(memory_space=pltpu.VMEM),
        scratch_shapes=[
            pltpu.SMEM(send_list.shape, jnp.int32),
            pltpu.SMEM(block_live.shape, jnp.int32),
            pltpu.SemaphoreType.DMA,
            pltpu.SemaphoreType.DMA((2,)),
        ],
        compiler_params=pltpu.CompilerParams(vmem_limit_bytes=VMEM),
        name="pack_live",
    )(send_list, block_live, kv_pool)


def stage(place, cand_rows, w_out):
    n = lax.axis_size("mp")
    rows, width = cand_rows.shape
    depth = w_out.shape[0]
    half = depth // 2
    total = rows + half + (n // 2 - 1) * depth

    def body(place_ref, rows_ref, w_ref, up_ref, down_ref, sem):
        def weights(k):
            start = pl.multiple_of(lax.rem(place_ref[0] + (k + n), n) * width, width)
            return w_ref.at[:, pl.ds(start, width)]

        copies = [
            (rows_ref, up_ref.at[pl.ds(half, rows)]),
            (rows_ref, down_ref.at[pl.ds(0, rows)]),
            (weights(n // 2).at[pl.ds(0, half)], up_ref.at[pl.ds(0, half)]),
            (weights(n // 2).at[pl.ds(half, half)], down_ref.at[pl.ds(rows, half)]),
        ]
        for k in range(1, n // 2):
            at = pl.ds(total - k * depth, depth)
            copies += [(weights(k), up_ref.at[at]), (weights(-k), down_ref.at[at])]
        copies = [pltpu.make_async_copy(a, b, sem.at[i]) for i, (a, b) in enumerate(copies)]
        for copy in copies:
            copy.start()
        for copy in copies:
            copy.wait()

    hbm = pl.BlockSpec(memory_space=pltpu.HBM)
    vmem = pl.BlockSpec(memory_space=pltpu.VMEM)
    shape = jax.ShapeDtypeStruct((total, width), BF16)
    return pl.pallas_call(
        body,
        out_shape=(shape, shape),
        in_specs=[pl.BlockSpec(memory_space=pltpu.SMEM), hbm, hbm],
        out_specs=(vmem, vmem),
        scratch_shapes=[pltpu.SemaphoreType.DMA((n + 2,))],
        compiler_params=pltpu.CompilerParams(vmem_limit_bytes=VMEM),
        name="stage",
    )(place, cand_rows, w_out)


def feature_rings(place, cand_rows, w_out):
    n = lax.axis_size("mp")
    rows = cand_rows.shape[0]
    depth = w_out.shape[0]
    half = depth // 2
    up = [(i, (i + 1) % n) for i in range(n)]
    down = [(i, (i - 1) % n) for i in range(n)]
    a, b = stage(place, cand_rows, w_out)
    ups, downs = [], []
    for k in range(n // 2 - 1):
        a = lax.ppermute(a, "mp", up)
        b = lax.ppermute(b, "mp", down)
        ups.append(a)
        downs.append(b)
        if k < n // 2 - 2:
            a, b = a[:-depth], b[:-depth]
    a = lax.ppermute(a[: half + rows // 2], "mp", up)
    b = lax.ppermute(b[rows // 2 : rows + half], "mp", down)
    return ups + [a], downs + [b]


def ring_gather(x, axis):
    n = lax.axis_size(axis)
    up = [(i, (i + 1) % n) for i in range(n)]
    down = [(i, (i - 1) % n) for i in range(n)]
    got = [x]
    left = right = x
    for _ in range(n // 2 - 1):
        left = lax.ppermute(left, axis, up)
        right = lax.ppermute(right, axis, down)
        got += [right, left]
    half = x.shape[0] // 2
    top = lax.ppermute(left[:half], axis, up)
    bottom = lax.ppermute(right[half:], axis, down)
    return got, top, bottom


def offsets(n):
    order = [0]
    for s in range(1, n // 2):
        order += [s, -s]
    return order + [n // 2]


def project(place, cand_rows, w_out, ups, downs, w_in, scale):
    n = lax.axis_size("mp")
    rows, width = cand_rows.shape
    depth = w_out.shape[0]
    half = depth // 2
    cols = w_in.shape[1]
    tile = rows // 4
    far = n // 2

    def body(*refs):
        place_ref, rows_ref, w_out_ref, w_in_hbm = refs[:4]
        up_refs, down_refs = refs[4 : 4 + far], refs[4 + far : 4 + 2 * far]
        gate_ref, query_ref, w_mine_ref, x_ref, w_in_ref, sem = refs[4 + 2 * far :]

        def spot(k):
            return lax.rem(place_ref[0] + (k + n), n)

        def columns(k):
            return pl.ds(pl.multiple_of(spot(k) * width, width), width)

        def weight_rows(k, start, size):
            return w_mine_ref.at[pl.ds(pl.multiple_of(spot(k) * depth + start, half), size)]

        copies = [
            (w_in_hbm, w_in_ref),
            (rows_ref, x_ref.at[:, columns(0)]),
            (w_out_ref.at[:, columns(0)], weight_rows(0, 0, depth)),
        ]
        for k in range(1, far):
            last = pl.ds(rows + half + (far - 1 - k) * depth, depth)
            copies += [
                (up_refs[k - 1].at[pl.ds(half, rows)], x_ref.at[:, columns(-k)]),
                (up_refs[k - 1].at[last], weight_rows(-k, 0, depth)),
                (down_refs[k - 1].at[pl.ds(0, rows)], x_ref.at[:, columns(k)]),
                (down_refs[k - 1].at[last], weight_rows(k, 0, depth)),
            ]
        top, bottom = pl.ds(0, rows // 2), pl.ds(rows // 2, rows // 2)
        copies += [
            (up_refs[-1].at[pl.ds(half, rows // 2)], x_ref.at[top, columns(far)]),
            (up_refs[-1].at[pl.ds(0, half)], weight_rows(far, 0, half)),
            (down_refs[-1].at[pl.ds(0, rows // 2)], x_ref.at[bottom, columns(far)]),
            (down_refs[-1].at[pl.ds(rows // 2, half)], weight_rows(far, half, half)),
        ]
        copies = [pltpu.make_async_copy(a, b, sem.at[i]) for i, (a, b) in enumerate(copies)]
        for copy in copies:
            copy.start()
        for copy in copies:
            copy.wait()
        for t in range(rows // tile):
            here = pl.ds(t * tile, tile)
            total = jnp.dot(x_ref[here, :], w_in_ref[...], preferred_element_type=F32)
            gate = total[:, : cols // 2]
            query = total[:, cols // 2 :]
            gate_ref[here, :] = gate / (1.0 + jnp.exp(-gate))
            query_ref[here, :] = (query / (1.0 + jnp.exp(-query)) * scale).astype(BF16)

    vmem = pl.BlockSpec(memory_space=pltpu.VMEM)
    hbm = pl.BlockSpec(memory_space=pltpu.HBM)
    return pl.pallas_call(
        body,
        out_shape=(
            jax.ShapeDtypeStruct((rows, cols // 2), F32),
            jax.ShapeDtypeStruct((rows, cols // 2), BF16),
            jax.ShapeDtypeStruct((n * depth, width), BF16),
        ),
        in_specs=[pl.BlockSpec(memory_space=pltpu.SMEM)] + [hbm] * (3 + 2 * far),
        out_specs=(vmem, vmem, vmem),
        scratch_shapes=[
            pltpu.VMEM((rows, n * width), BF16),
            pltpu.VMEM(w_in.shape, BF16),
            pltpu.SemaphoreType.DMA((3 + 4 * far,)),
        ],
        compiler_params=pltpu.CompilerParams(vmem_limit_bytes=VMEM),
        cost_estimate=pl.CostEstimate(
            flops=2 * rows * n * width * cols, bytes_accessed=4 << 20, transcendentals=rows * cols
        ),
        name="project",
    )(place, cand_rows, w_out, w_in, *ups, *downs)


def attend(part, count, query, gate, history):
    at, rows = part
    head = query.shape[1]
    owners, fields, block_len, _ = history.shape
    group = 4
    tile = 256

    def body(count_ref, query_ref, gate_ref, history_ref, out_ref, total_ref):
        step = pl.program_id(0)
        live = jnp.clip(count_ref[0] - at, 0, rows)
        tiles = lax.div(live + (tile - 1), tile)

        @pl.when(step == 0)
        def _():
            total_ref[...] = jnp.zeros_like(total_ref)

        def one(t, _):
            here = pl.ds(pl.multiple_of(t * tile, tile), tile)
            query = query_ref[pl.ds(pl.multiple_of(at + t * tile, tile), tile), :]
            total = total_ref[here, :]
            for k in range(fields // 2):
                keys = history_ref[:, 2 * k].reshape(group * block_len, head)
                values = history_ref[:, 2 * k + 1].reshape(group * block_len, head)
                half = lax.dot_general(
                    query, keys, (((1,), (1,)), ((), ())), preferred_element_type=F32
                )
                weight = (half * jnp.tanh(half) + half).astype(BF16)
                total += jnp.dot(weight, values, preferred_element_type=F32)
            total_ref[here, :] = total
            return 0

        lax.fori_loop(0, tiles, one, 0)

        @pl.when(step == pl.num_programs(0) - 1)
        def _():
            total = total_ref[...]
            center = total - jnp.mean(total, axis=-1, keepdims=True)
            variance = jnp.mean(center * center, axis=-1, keepdims=True)
            scaled = center * lax.rsqrt(variance + 1e-05)
            out_ref[...] = (scaled * gate_ref[pl.ds(at, rows), :]).astype(BF16)

    vmem = pl.BlockSpec(memory_space=pltpu.VMEM)
    keys_all = owners * block_len * fields // 2
    return pl.pallas_call(
        body,
        grid=(owners // group,),
        out_shape=jax.ShapeDtypeStruct((rows, head), BF16),
        in_specs=[
            pl.BlockSpec(memory_space=pltpu.SMEM),
            vmem,
            vmem,
            pl.BlockSpec((group, fields, block_len, head), lambda i: (i, 0, 0, 0)),
        ],
        out_specs=vmem,
        scratch_shapes=[pltpu.VMEM((rows, head), F32)],
        compiler_params=pltpu.CompilerParams(vmem_limit_bytes=VMEM),
        cost_estimate=pl.CostEstimate(
            flops=4 * rows * keys_all * head,
            bytes_accessed=4 << 20,
            transcendentals=rows * keys_all,
        ),
        name="attend",
    )(count, query, gate, history)


def output(place, count, cand_rows, parts, w_mine):
    n = lax.axis_size("mp")
    rows, width = cand_rows.shape
    size = rows // len(parts)
    tile = min(256, size // 2)
    steps = offsets(n)
    each = n + 1

    def body(*refs):
        place_ref, count_ref, rows_ref, w_ref = refs[:4]
        out_ref = refs[-1]
        weights = []
        for s in steps:
            start = lax.rem(place_ref[0] + (s + n), n) * width
            weights.append(w_ref[pl.ds(pl.multiple_of(start, width), width), :])
        for p in range(len(parts)):
            block_refs = refs[4 + p * each : 4 + (p + 1) * each]
            top_ref, bottom_ref = block_refs[-2:]
            for t in range(size // tile):
                local = pl.ds(t * tile, tile)
                here = pl.ds(p * size + t * tile, tile)
                total = rows_ref[here, :].astype(F32)
                for ref, w in zip(block_refs[:-2], weights):
                    total += jnp.dot(ref[local, :], w, preferred_element_type=F32)
                far = top_ref if t * tile < size // 2 else bottom_ref
                last = far[pl.ds((t * tile) % (size // 2), tile), :]
                total += jnp.dot(last, weights[-1], preferred_element_type=F32)
                index = lax.broadcasted_iota(jnp.int32, (tile, width), 0) + (p * size + t * tile)
                out_ref[here, :] = jnp.where(index < count_ref[0], total, 0.0).astype(BF16)

    vmem = pl.BlockSpec(memory_space=pltpu.VMEM)
    smem = pl.BlockSpec(memory_space=pltpu.SMEM)
    blocks = []
    for got, top, bottom in parts:
        blocks += got + [top, bottom]
    return pl.pallas_call(
        body,
        out_shape=jax.ShapeDtypeStruct((rows, width), BF16),
        in_specs=[smem, smem] + [vmem] * (2 + len(blocks)),
        out_specs=vmem,
        compiler_params=pltpu.CompilerParams(vmem_limit_bytes=VMEM),
        cost_estimate=pl.CostEstimate(
            flops=2 * rows * n * width * width, bytes_accessed=4 << 20, transcendentals=0
        ),
        name="output",
    )(place, count, cand_rows, w_mine, *blocks)


def per_device(cand_rows, w_in, w_out, kv_pool, send_list, block_live, cand_count):
    rows = cand_rows.shape[0]
    head = kv_pool.shape[3]
    w_out = w_out.reshape(-1, w_out.shape[2])
    w_in = w_in.reshape(w_in.shape[0], -1)
    place = lax.axis_index("mp").astype(jnp.int32).reshape(1)
    packed = pack_live(send_list, block_live, kv_pool)
    history = lax.all_to_all(packed, "cache", split_axis=0, concat_axis=0, tiled=True)

    cand_later, _ = lax.optimization_barrier((cand_rows, packed))
    ups, downs = feature_rings(place, cand_later, w_out)
    gate, query, w_mine = project(
        place, cand_rows, w_out, ups, downs, w_in, 0.5 * head ** (-0.5)
    )
    size = rows // PARTS
    parts = []
    for p in range(PARTS):
        gated = attend((p * size, size), cand_count, query, gate, history)
        parts.append(ring_gather(gated, "mp"))
    return output(place, cand_count, cand_rows, parts, w_mine)


def solution(mesh):
    return jax.shard_map(
        per_device,
        mesh=mesh,
        in_specs=(
            P("cache", "mp"),
            P(None, "mp", None),
            P("mp", None, None),
            P(None, "cache", None, "mp"),
            P("cache", None),
            P("cache", None),
            P("cache"),
        ),
        out_specs=P("cache", "mp"),
        check_vma=False,
    )
```

```python
import jax
import jax.numpy as jnp
from jax import lax
from jax.experimental import pallas as pl
from jax.experimental.pallas import tpu as pltpu
from jax.sharding import PartitionSpec as P

BF16 = jnp.bfloat16
F32 = jnp.float32
VMEM = 16 * 1024 * 1024
MOST_VMEM = 60 * 1024 * 1024
LIVE = 2


def pack_live(send_list, block_live, kv_pool):
    pool = kv_pool.shape[1]
    tile = kv_pool.shape[2:]
    rankers = lax.axis_size("cache")
    slots = pool // rankers

    def body(send_hbm, live_hbm, pool_ref, out_ref, send_ref, live_ref, zero_ref, buf, list_sem, in_sem, out_sem):
        lists = [
            pltpu.make_async_copy(send_hbm, send_ref, list_sem.at[0]),
            pltpu.make_async_copy(live_hbm, live_ref, list_sem.at[1]),
        ]
        for copy in lists:
            copy.start()
        zero_ref[...] = jnp.zeros_like(zero_ref)
        for copy in lists:
            copy.wait()

        def fetch(r, _):
            seen = jnp.int32(0)
            blocks = [jnp.int32(0)] * LIVE
            for s in range(slots):
                live = live_ref[0, r * slots + s]
                for k in range(LIVE):
                    hit = jnp.logical_and(seen == k, live > 0)
                    blocks[k] = jnp.where(hit, send_ref[0, r * slots + s], blocks[k])
                seen = seen + live
            for k in range(LIVE):
                there = buf.at[r, pl.ds(2 * k, 2)]

                @pl.when(seen > k)
                def _():
                    pltpu.make_async_copy(pool_ref.at[:, blocks[k]], there, in_sem.at[r]).start()

                @pl.when(seen <= k)
                def _():
                    pltpu.make_async_copy(zero_ref, there, in_sem.at[r]).start()

            return 0

        def pass_on(r, _):
            pltpu.make_async_copy(buf.at[r], buf.at[r], in_sem.at[r]).wait()
            pltpu.make_async_copy(buf.at[r], out_ref.at[r], out_sem).start()
            return 0

        lax.fori_loop(0, rankers, fetch, 0, unroll=4)
        lax.fori_loop(0, rankers, pass_on, 0, unroll=4)
        pltpu.make_async_copy(buf, out_ref, out_sem).wait()

    hbm = pl.BlockSpec(memory_space=pl.ANY)
    return pl.pallas_call(
        body,
        out_shape=jax.ShapeDtypeStruct((rankers, 2 * LIVE) + tile, BF16),
        in_specs=[hbm, hbm, hbm],
        out_specs=hbm,
        scratch_shapes=[
            pltpu.SMEM(send_list.shape, jnp.int32),
            pltpu.SMEM(block_live.shape, jnp.int32),
            pltpu.VMEM((2,) + tile, BF16),
            pltpu.VMEM((rankers, 2 * LIVE) + tile, BF16),
            pltpu.SemaphoreType.DMA((2,)),
            pltpu.SemaphoreType.DMA((rankers,)),
            pltpu.SemaphoreType.DMA,
        ],
        compiler_params=pltpu.CompilerParams(vmem_limit_bytes=MOST_VMEM),
        name="pack_live",
    )(send_list, block_live, kv_pool)


def stage(place, cand_rows, w_out):
    n = lax.axis_size("mp")
    rows, width = cand_rows.shape
    depth = w_out.shape[0]
    half = depth // 2
    total = rows + half + (n // 2 - 1) * depth

    def body(place_ref, rows_ref, w_ref, up_ref, down_ref, sem):
        def weights(k):
            start = pl.multiple_of(lax.rem(place_ref[0] + (k + n), n) * width, width)
            return w_ref.at[:, pl.ds(start, width)]

        copies = [
            (rows_ref, up_ref.at[pl.ds(half, rows)]),
            (rows_ref, down_ref.at[pl.ds(0, rows)]),
            (weights(n // 2).at[pl.ds(0, half)], up_ref.at[pl.ds(0, half)]),
            (weights(n // 2).at[pl.ds(half, half)], down_ref.at[pl.ds(rows, half)]),
        ]
        for k in range(1, n // 2):
            at = pl.ds(total - k * depth, depth)
            copies += [(weights(k), up_ref.at[at]), (weights(-k), down_ref.at[at])]
        copies = [pltpu.make_async_copy(a, b, sem.at[i]) for i, (a, b) in enumerate(copies)]
        for copy in copies:
            copy.start()
        for copy in copies:
            copy.wait()

    hbm = pl.BlockSpec(memory_space=pltpu.HBM)
    vmem = pl.BlockSpec(memory_space=pltpu.VMEM)
    shape = jax.ShapeDtypeStruct((total, width), BF16)
    return pl.pallas_call(
        body,
        out_shape=(shape, shape),
        in_specs=[pl.BlockSpec(memory_space=pltpu.SMEM), hbm, hbm],
        out_specs=(vmem, vmem),
        scratch_shapes=[pltpu.SemaphoreType.DMA((n + 2,))],
        compiler_params=pltpu.CompilerParams(vmem_limit_bytes=VMEM),
        name="stage",
    )(place, cand_rows, w_out)


def feature_rings(place, cand_rows, w_out):
    n = lax.axis_size("mp")
    rows = cand_rows.shape[0]
    depth = w_out.shape[0]
    half = depth // 2
    up = [(i, (i + 1) % n) for i in range(n)]
    down = [(i, (i - 1) % n) for i in range(n)]
    a, b = stage(place, cand_rows, w_out)
    ups, downs = [], []
    for k in range(n // 2 - 1):
        a = lax.ppermute(a, "mp", up)
        b = lax.ppermute(b, "mp", down)
        ups.append(a)
        downs.append(b)
        if k < n // 2 - 2:
            a, b = a[:-depth], b[:-depth]
    a = lax.ppermute(a[: half + rows // 2], "mp", up)
    b = lax.ppermute(b[rows // 2 : rows + half], "mp", down)
    return ups + [a], downs + [b]


def ring_gather(x, axis):
    n = lax.axis_size(axis)
    up = [(i, (i + 1) % n) for i in range(n)]
    down = [(i, (i - 1) % n) for i in range(n)]
    got = [x]
    left = right = x
    for _ in range(n // 2 - 1):
        left = lax.ppermute(left, axis, up)
        right = lax.ppermute(right, axis, down)
        got += [right, left]
    half = x.shape[0] // 2
    top = lax.ppermute(left[:half], axis, up)
    bottom = lax.ppermute(right[half:], axis, down)
    return got, top, bottom


def columns(place_ref, distance, n, width):
    start = lax.rem(place_ref[0] + (distance + n), n) * width
    return pl.ds(pl.multiple_of(start, width), width)


def offsets(n):
    order = [0]
    for s in range(1, n // 2):
        order += [s, -s]
    return order + [n // 2]


def project(place, cand_rows, w_out, ups, downs, w_in, scale):
    n = lax.axis_size("mp")
    rows, width = cand_rows.shape
    depth = w_out.shape[0]
    half = depth // 2
    cols = w_in.shape[1]
    tile = rows // 4
    far = n // 2

    def body(*refs):
        place_ref, rows_ref, w_out_ref, w_in_hbm = refs[:4]
        up_refs, down_refs = refs[4 : 4 + far], refs[4 + far : 4 + 2 * far]
        gate_ref, query_ref, w_mine_ref, x_ref, w_in_ref, sem = refs[4 + 2 * far :]

        def spot(k):
            return lax.rem(place_ref[0] + (k + n), n)

        def columns(k):
            return pl.ds(pl.multiple_of(spot(k) * width, width), width)

        def weight_rows(k, start, size):
            return w_mine_ref.at[pl.ds(pl.multiple_of(spot(k) * depth + start, half), size)]

        copies = [
            (w_in_hbm, w_in_ref),
            (rows_ref, x_ref.at[:, columns(0)]),
            (w_out_ref.at[:, columns(0)], weight_rows(0, 0, depth)),
        ]
        for k in range(1, far):
            last = pl.ds(rows + half + (far - 1 - k) * depth, depth)
            copies += [
                (up_refs[k - 1].at[pl.ds(half, rows)], x_ref.at[:, columns(-k)]),
                (up_refs[k - 1].at[last], weight_rows(-k, 0, depth)),
                (down_refs[k - 1].at[pl.ds(0, rows)], x_ref.at[:, columns(k)]),
                (down_refs[k - 1].at[last], weight_rows(k, 0, depth)),
            ]
        top, bottom = pl.ds(0, rows // 2), pl.ds(rows // 2, rows // 2)
        copies += [
            (up_refs[-1].at[pl.ds(half, rows // 2)], x_ref.at[top, columns(far)]),
            (up_refs[-1].at[pl.ds(0, half)], weight_rows(far, 0, half)),
            (down_refs[-1].at[pl.ds(0, rows // 2)], x_ref.at[bottom, columns(far)]),
            (down_refs[-1].at[pl.ds(rows // 2, half)], weight_rows(far, half, half)),
        ]
        copies = [pltpu.make_async_copy(a, b, sem.at[i]) for i, (a, b) in enumerate(copies)]
        for copy in copies:
            copy.start()
        for copy in copies:
            copy.wait()
        for t in range(rows // tile):
            here = pl.ds(t * tile, tile)
            total = jnp.dot(x_ref[here, :], w_in_ref[...], preferred_element_type=F32)
            gate = total[:, : cols // 2]
            query = total[:, cols // 2 :]
            gate_ref[here, :] = gate / (1.0 + jnp.exp(-gate))
            query_ref[here, :] = (query / (1.0 + jnp.exp(-query)) * scale).astype(BF16)

    vmem = pl.BlockSpec(memory_space=pltpu.VMEM)
    hbm = pl.BlockSpec(memory_space=pltpu.HBM)
    return pl.pallas_call(
        body,
        out_shape=(
            jax.ShapeDtypeStruct((rows, cols // 2), F32),
            jax.ShapeDtypeStruct((rows, cols // 2), BF16),
            jax.ShapeDtypeStruct((n * depth, width), BF16),
        ),
        in_specs=[pl.BlockSpec(memory_space=pltpu.SMEM)] + [hbm] * (3 + 2 * far),
        out_specs=(vmem, vmem, vmem),
        scratch_shapes=[
            pltpu.VMEM((rows, n * width), BF16),
            pltpu.VMEM(w_in.shape, BF16),
            pltpu.SemaphoreType.DMA((3 + 4 * far,)),
        ],
        compiler_params=pltpu.CompilerParams(vmem_limit_bytes=VMEM),
        cost_estimate=pl.CostEstimate(
            flops=2 * rows * n * width * cols, bytes_accessed=4 << 20, transcendentals=rows * cols
        ),
        name="project",
    )(place, cand_rows, w_out, w_in, *ups, *downs)


def attend(count, query, gate, history):
    rows, head = query.shape
    owners, fields, block_len, _ = history.shape
    keys = 4
    groups = [(0, owners // 4), (owners // 4, owners - owners // 4)]
    part = rows // 2

    def body(count_ref, query_hbm, gate_hbm, history_hbm, out_ref, query_ref, gate_ref, buf, total_ref, sem, own_sem):
        get_query = pltpu.make_async_copy(query_hbm, query_ref, own_sem.at[0])
        get_gate = pltpu.make_async_copy(gate_hbm, gate_ref, own_sem.at[1])
        get_query.start()
        copies = []
        for i, (start, size) in enumerate(groups):
            here = pl.ds(start, size)
            copies.append(pltpu.make_async_copy(history_hbm.at[here], buf.at[here], sem.at[i]))
        for copy in copies:
            copy.start()
        get_gate.start()
        total_ref[...] = jnp.zeros_like(total_ref)
        get_query.wait()
        for copy, (start, size) in zip(copies, groups):
            copy.wait()
            for p in range(rows // part):
                here = pl.ds(p * part, part)

                @pl.when(count_ref[0] > p * part)
                def _():
                    query = query_ref[here, :]
                    total = total_ref[here, :]

                    def score(unit):
                        k, o = unit
                        key = buf[o : o + keys, 2 * k].reshape(keys * block_len, head)
                        return lax.dot_general(
                            query, key, (((1,), (1,)), ((), ())), preferred_element_type=F32
                        )

                    units = [
                        (k, o) for o in range(start, start + size, keys) for k in range(fields // 2)
                    ]
                    ahead = score(units[0])
                    for i, (k, o) in enumerate(units):
                        half = ahead
                        if i + 1 < len(units):
                            ahead = score(units[i + 1])
                        weight = (half * jnp.tanh(half) + half).astype(BF16)
                        value = buf[o : o + keys, 2 * k + 1].reshape(keys * block_len, head)
                        total += jnp.dot(weight, value, preferred_element_type=F32)
                    total_ref[here, :] = total

        get_gate.wait()
        for p in range(rows // part):
            here = pl.ds(p * part, part)

            @pl.when(count_ref[0] > p * part)
            def _():
                total = total_ref[here, :]
                center = total - jnp.mean(total, axis=-1, keepdims=True)
                variance = jnp.mean(center * center, axis=-1, keepdims=True)
                scaled = center * lax.rsqrt(variance + 1e-05)
                out_ref[here, :] = (scaled * gate_ref[here, :]).astype(BF16)

            @pl.when(count_ref[0] <= p * part)
            def _():
                out_ref[here, :] = jnp.zeros((part, head), BF16)

    hbm = pl.BlockSpec(memory_space=pl.ANY)
    keys_all = owners * block_len * fields // 2
    return pl.pallas_call(
        body,
        out_shape=jax.ShapeDtypeStruct((rows, head), BF16),
        in_specs=[pl.BlockSpec(memory_space=pltpu.SMEM), hbm, hbm, hbm],
        out_specs=pl.BlockSpec(memory_space=pltpu.VMEM),
        scratch_shapes=[
            pltpu.VMEM((rows, head), BF16),
            pltpu.VMEM((rows, head), F32),
            pltpu.VMEM(history.shape, BF16),
            pltpu.VMEM((rows, head), F32),
            pltpu.SemaphoreType.DMA((len(groups),)),
            pltpu.SemaphoreType.DMA((2,)),
        ],
        compiler_params=pltpu.CompilerParams(vmem_limit_bytes=MOST_VMEM),
        cost_estimate=pl.CostEstimate(
            flops=4 * rows * keys_all * head,
            bytes_accessed=4 << 20,
            transcendentals=rows * keys_all,
        ),
        name="attend",
    )(count, query, gate, history)


def output_near(place, cand_rows, blocks, w_mine):
    n = lax.axis_size("mp")
    rows, width = cand_rows.shape
    tile = rows // 4
    steps = offsets(n)[: len(blocks)]

    def body(*refs):
        place_ref, rows_ref, w_ref = refs[:3]
        block_refs, out_ref = refs[3:-1], refs[-1]
        weights = [w_ref[columns(place_ref, s, n, width), :] for s in steps]
        for t in range(rows // tile):
            here = pl.ds(t * tile, tile)
            total = rows_ref[here, :].astype(F32)
            for ref, w in zip(block_refs, weights):
                total += jnp.dot(ref[here, :], w, preferred_element_type=F32)
            out_ref[here, :] = total

    vmem = pl.BlockSpec(memory_space=pltpu.VMEM)
    smem = pl.BlockSpec(memory_space=pltpu.SMEM)
    return pl.pallas_call(
        body,
        out_shape=jax.ShapeDtypeStruct((rows, width), F32),
        in_specs=[smem] + [vmem] * (2 + len(blocks)),
        out_specs=vmem,
        compiler_params=pltpu.CompilerParams(vmem_limit_bytes=VMEM),
        cost_estimate=pl.CostEstimate(
            flops=2 * rows * len(blocks) * width * width, bytes_accessed=2 << 20, transcendentals=0
        ),
        name="output_near",
    )(place, cand_rows, w_mine, *blocks)


def output(place, count, near, blocks, top, bottom, w_mine):
    n = lax.axis_size("mp")
    rows, width = near.shape
    tile = rows // 4
    steps = offsets(n)[-1 - len(blocks) :]

    def body(*refs):
        place_ref, count_ref, near_ref, w_ref = refs[:4]
        block_refs = refs[4:-3]
        top_ref, bottom_ref, out_ref = refs[-3:]
        weights = [w_ref[columns(place_ref, s, n, width), :] for s in steps]
        for t in range(rows // tile):
            here = pl.ds(t * tile, tile)
            total = near_ref[here, :]
            for ref, w in zip(block_refs, weights):
                total += jnp.dot(ref[here, :], w, preferred_element_type=F32)
            far = top_ref if t * tile < rows // 2 else bottom_ref
            last = far[pl.ds((t * tile) % (rows // 2), tile), :]
            total += jnp.dot(last, weights[-1], preferred_element_type=F32)
            index = lax.broadcasted_iota(jnp.int32, (tile, width), 0) + t * tile
            out_ref[here, :] = jnp.where(index < count_ref[0], total, 0.0).astype(BF16)

    vmem = pl.BlockSpec(memory_space=pltpu.VMEM)
    smem = pl.BlockSpec(memory_space=pltpu.SMEM)
    return pl.pallas_call(
        body,
        out_shape=jax.ShapeDtypeStruct((rows, width), BF16),
        in_specs=[smem, smem] + [vmem] * (4 + len(blocks)),
        out_specs=vmem,
        compiler_params=pltpu.CompilerParams(vmem_limit_bytes=VMEM),
        cost_estimate=pl.CostEstimate(
            flops=2 * rows * (len(blocks) + 1) * width * width,
            bytes_accessed=2 << 20,
            transcendentals=0,
        ),
        name="output",
    )(place, count, near, w_mine, *blocks, top, bottom)


def per_device(cand_rows, w_in, w_out, kv_pool, send_list, block_live, cand_count):
    head = kv_pool.shape[3]
    w_out = w_out.reshape(-1, w_out.shape[2])
    w_in = w_in.reshape(w_in.shape[0], -1)
    place = lax.axis_index("mp").astype(jnp.int32).reshape(1)
    packed = pack_live(send_list, block_live, kv_pool)
    history = lax.all_to_all(packed, "cache", split_axis=0, concat_axis=0, tiled=True)

    cand_later, _ = lax.optimization_barrier((cand_rows, packed))
    ups, downs = feature_rings(place, cand_later, w_out)
    gate, query, w_mine = project(
        place, cand_rows, w_out, ups, downs, w_in, 0.5 * head ** (-0.5)
    )
    gated = attend(cand_count, query, gate, history)
    heads, top, bottom = ring_gather(gated, "mp")
    near = output_near(place, cand_rows, heads[:-2], w_mine)
    return output(place, cand_count, near, heads[-2:], top, bottom, w_mine)


def solution(mesh):
    return jax.shard_map(
        per_device,
        mesh=mesh,
        in_specs=(
            P("cache", "mp"),
            P(None, "mp", None),
            P("mp", None, None),
            P(None, "cache", None, "mp"),
            P("cache", None),
            P("cache", None),
            P("cache"),
        ),
        out_specs=P("cache", "mp"),
        check_vma=False,
    )
```

```python
import jax
import jax.numpy as jnp
from jax import lax
from jax.experimental import pallas as pl
from jax.experimental.pallas import tpu as pltpu
from jax.sharding import PartitionSpec as P

BF16 = jnp.bfloat16
F32 = jnp.float32
VMEM = 16 * 1024 * 1024
MOST_VMEM = 60 * 1024 * 1024
LIVE = 2


def pack_live(send_list, block_live, kv_pool):
    pool = kv_pool.shape[1]
    tile = kv_pool.shape[2:]
    rankers = lax.axis_size("cache")
    slots = pool // rankers

    def body(send_hbm, live_hbm, pool_ref, out_ref, send_ref, live_ref, zero_ref, buf, list_sem, in_sem, out_sem):
        lists = [
            pltpu.make_async_copy(send_hbm, send_ref, list_sem.at[0]),
            pltpu.make_async_copy(live_hbm, live_ref, list_sem.at[1]),
        ]
        for copy in lists:
            copy.start()
        zero_ref[...] = jnp.zeros_like(zero_ref)
        for copy in lists:
            copy.wait()

        def fetch(r, _):
            seen = jnp.int32(0)
            blocks = [jnp.int32(0)] * LIVE
            for s in range(slots):
                live = live_ref[0, r * slots + s]
                for k in range(LIVE):
                    hit = jnp.logical_and(seen == k, live > 0)
                    blocks[k] = jnp.where(hit, send_ref[0, r * slots + s], blocks[k])
                seen = seen + live
            for k in range(LIVE):
                there = buf.at[r, pl.ds(2 * k, 2)]

                @pl.when(seen > k)
                def _():
                    pltpu.make_async_copy(pool_ref.at[:, blocks[k]], there, in_sem.at[r]).start()

                @pl.when(seen <= k)
                def _():
                    pltpu.make_async_copy(zero_ref, there, in_sem.at[r]).start()

            return 0

        def pass_on(r, _):
            pltpu.make_async_copy(buf.at[r], buf.at[r], in_sem.at[r]).wait()
            pltpu.make_async_copy(buf.at[r], out_ref.at[r], out_sem).start()
            return 0

        lax.fori_loop(0, rankers, fetch, 0, unroll=4)
        lax.fori_loop(0, rankers, pass_on, 0, unroll=4)
        pltpu.make_async_copy(buf, out_ref, out_sem).wait()

    hbm = pl.BlockSpec(memory_space=pl.ANY)
    return pl.pallas_call(
        body,
        out_shape=jax.ShapeDtypeStruct((rankers, 2 * LIVE) + tile, BF16),
        in_specs=[hbm, hbm, hbm],
        out_specs=hbm,
        scratch_shapes=[
            pltpu.SMEM(send_list.shape, jnp.int32),
            pltpu.SMEM(block_live.shape, jnp.int32),
            pltpu.VMEM((2,) + tile, BF16),
            pltpu.VMEM((rankers, 2 * LIVE) + tile, BF16),
            pltpu.SemaphoreType.DMA((2,)),
            pltpu.SemaphoreType.DMA((rankers,)),
            pltpu.SemaphoreType.DMA,
        ],
        compiler_params=pltpu.CompilerParams(vmem_limit_bytes=MOST_VMEM),
        name="pack_live",
    )(send_list, block_live, kv_pool)


def stage(place, cand_rows, w_out):
    n = lax.axis_size("mp")
    rows, width = cand_rows.shape
    depth = w_out.shape[0]
    half = depth // 2
    total = rows + half + (n // 2 - 1) * depth

    def body(place_ref, rows_ref, w_ref, up_ref, down_ref, sem):
        def weights(k):
            start = pl.multiple_of(lax.rem(place_ref[0] + (k + n), n) * width, width)
            return w_ref.at[:, pl.ds(start, width)]

        copies = [
            (rows_ref, up_ref.at[pl.ds(half, rows)]),
            (rows_ref, down_ref.at[pl.ds(0, rows)]),
            (weights(n // 2).at[pl.ds(0, half)], up_ref.at[pl.ds(0, half)]),
            (weights(n // 2).at[pl.ds(half, half)], down_ref.at[pl.ds(rows, half)]),
        ]
        for k in range(1, n // 2):
            at = pl.ds(total - k * depth, depth)
            copies += [(weights(k), up_ref.at[at]), (weights(-k), down_ref.at[at])]
        copies = [pltpu.make_async_copy(a, b, sem.at[i]) for i, (a, b) in enumerate(copies)]
        for copy in copies:
            copy.start()
        for copy in copies:
            copy.wait()

    hbm = pl.BlockSpec(memory_space=pltpu.HBM)
    vmem = pl.BlockSpec(memory_space=pltpu.VMEM)
    shape = jax.ShapeDtypeStruct((total, width), BF16)
    return pl.pallas_call(
        body,
        out_shape=(shape, shape),
        in_specs=[pl.BlockSpec(memory_space=pltpu.SMEM), hbm, hbm],
        out_specs=(vmem, vmem),
        scratch_shapes=[pltpu.SemaphoreType.DMA((n + 2,))],
        compiler_params=pltpu.CompilerParams(vmem_limit_bytes=VMEM),
        name="stage",
    )(place, cand_rows, w_out)


def feature_rings(place, cand_rows, w_out):
    n = lax.axis_size("mp")
    rows = cand_rows.shape[0]
    depth = w_out.shape[0]
    half = depth // 2
    up = [(i, (i + 1) % n) for i in range(n)]
    down = [(i, (i - 1) % n) for i in range(n)]
    a, b = stage(place, cand_rows, w_out)
    ups, downs = [], []
    for k in range(n // 2 - 1):
        a = lax.ppermute(a, "mp", up)
        b = lax.ppermute(b, "mp", down)
        ups.append(a)
        downs.append(b)
        if k < n // 2 - 2:
            a, b = a[:-depth], b[:-depth]
    a = lax.ppermute(a[: half + rows // 2], "mp", up)
    b = lax.ppermute(b[rows // 2 : rows + half], "mp", down)
    return ups + [a], downs + [b]


def ring_gather(x, axis):
    n = lax.axis_size(axis)
    up = [(i, (i + 1) % n) for i in range(n)]
    down = [(i, (i - 1) % n) for i in range(n)]
    got = [x]
    left = right = x
    for _ in range(n // 2 - 1):
        left = lax.ppermute(left, axis, up)
        right = lax.ppermute(right, axis, down)
        got += [right, left]
    half = x.shape[0] // 2
    top = lax.ppermute(left[:half], axis, up)
    bottom = lax.ppermute(right[half:], axis, down)
    return got, top, bottom


def columns(place_ref, distance, n, width):
    start = lax.rem(place_ref[0] + (distance + n), n) * width
    return pl.ds(pl.multiple_of(start, width), width)


def offsets(n):
    order = [0]
    for s in range(1, n // 2):
        order += [s, -s]
    return order + [n // 2]


def project(place, cand_rows, w_out, ups, downs, w_in, scale):
    n = lax.axis_size("mp")
    rows, width = cand_rows.shape
    depth = w_out.shape[0]
    half = depth // 2
    cols = w_in.shape[1]
    tile = rows // 4
    far = n // 2

    def body(*refs):
        place_ref, rows_ref, w_out_ref, w_in_hbm = refs[:4]
        up_refs, down_refs = refs[4 : 4 + far], refs[4 + far : 4 + 2 * far]
        gate_ref, query_ref, w_mine_ref, x_ref, w_in_ref, sem = refs[4 + 2 * far :]

        def spot(k):
            return lax.rem(place_ref[0] + (k + n), n)

        def columns(k):
            return pl.ds(pl.multiple_of(spot(k) * width, width), width)

        def weight_rows(k, start, size):
            return w_mine_ref.at[pl.ds(pl.multiple_of(spot(k) * depth + start, half), size)]

        copies = [
            (w_in_hbm, w_in_ref),
            (rows_ref, x_ref.at[:, columns(0)]),
            (w_out_ref.at[:, columns(0)], weight_rows(0, 0, depth)),
        ]
        for k in range(1, far):
            last = pl.ds(rows + half + (far - 1 - k) * depth, depth)
            copies += [
                (up_refs[k - 1].at[pl.ds(half, rows)], x_ref.at[:, columns(-k)]),
                (up_refs[k - 1].at[last], weight_rows(-k, 0, depth)),
                (down_refs[k - 1].at[pl.ds(0, rows)], x_ref.at[:, columns(k)]),
                (down_refs[k - 1].at[last], weight_rows(k, 0, depth)),
            ]
        top, bottom = pl.ds(0, rows // 2), pl.ds(rows // 2, rows // 2)
        copies += [
            (up_refs[-1].at[pl.ds(half, rows // 2)], x_ref.at[top, columns(far)]),
            (up_refs[-1].at[pl.ds(0, half)], weight_rows(far, 0, half)),
            (down_refs[-1].at[pl.ds(0, rows // 2)], x_ref.at[bottom, columns(far)]),
            (down_refs[-1].at[pl.ds(rows // 2, half)], weight_rows(far, half, half)),
        ]
        copies = [pltpu.make_async_copy(a, b, sem.at[i]) for i, (a, b) in enumerate(copies)]
        for copy in copies:
            copy.start()
        for copy in copies:
            copy.wait()
        for t in range(rows // tile):
            here = pl.ds(t * tile, tile)
            total = jnp.dot(x_ref[here, :], w_in_ref[...], preferred_element_type=F32)
            gate = total[:, : cols // 2]
            query = total[:, cols // 2 :]
            gate_ref[here, :] = gate / (1.0 + jnp.exp(-gate))
            query_ref[here, :] = (query / (1.0 + jnp.exp(-query)) * scale).astype(BF16)

    vmem = pl.BlockSpec(memory_space=pltpu.VMEM)
    hbm = pl.BlockSpec(memory_space=pltpu.HBM)
    return pl.pallas_call(
        body,
        out_shape=(
            jax.ShapeDtypeStruct((rows, cols // 2), F32),
            jax.ShapeDtypeStruct((rows, cols // 2), BF16),
            jax.ShapeDtypeStruct((n * depth, width), BF16),
        ),
        in_specs=[pl.BlockSpec(memory_space=pltpu.SMEM)] + [hbm] * (3 + 2 * far),
        out_specs=(vmem, vmem, vmem),
        scratch_shapes=[
            pltpu.VMEM((rows, n * width), BF16),
            pltpu.VMEM(w_in.shape, BF16),
            pltpu.SemaphoreType.DMA((3 + 4 * far,)),
        ],
        compiler_params=pltpu.CompilerParams(vmem_limit_bytes=VMEM),
        cost_estimate=pl.CostEstimate(
            flops=2 * rows * n * width * cols, bytes_accessed=4 << 20, transcendentals=rows * cols
        ),
        name="project",
    )(place, cand_rows, w_out, w_in, *ups, *downs)


def attend(count, query, gate, history):
    rows, head = query.shape
    owners, fields, block_len, _ = history.shape
    keys = 4
    groups = 2
    size = owners // groups
    part = rows // 2

    def body(count_ref, query_hbm, gate_hbm, history_hbm, out_ref, query_ref, gate_ref, buf, total_ref, sem, own_sem):
        get_query = pltpu.make_async_copy(query_hbm, query_ref, own_sem.at[0])
        get_gate = pltpu.make_async_copy(gate_hbm, gate_ref, own_sem.at[1])
        get_query.start()

        def get_group(g):
            here = pl.ds(g * size, size)
            return pltpu.make_async_copy(history_hbm.at[here], buf.at[here], sem.at[g])

        for g in range(groups):
            get_group(g).start()
        get_gate.start()
        total_ref[...] = jnp.zeros_like(total_ref)
        get_query.wait()
        parts = lax.div(count_ref[0] + (part - 1), part)

        def one_group(g, _):
            get_group(g).wait()

            def one_part(p, _):
                here = pl.ds(pl.multiple_of(p * part, part), part)
                query = query_ref[here, :]
                total = total_ref[here, :]

                def score(unit):
                    k, o = unit
                    key = buf[pl.ds(g * size + o, keys), 2 * k].reshape(keys * block_len, head)
                    return lax.dot_general(
                        query, key, (((1,), (1,)), ((), ())), preferred_element_type=F32
                    )

                units = [(k, o) for o in range(0, size, keys) for k in range(fields // 2)]
                ahead = score(units[0])
                for i, (k, o) in enumerate(units):
                    half = ahead
                    if i + 1 < len(units):
                        ahead = score(units[i + 1])
                    weight = (half * jnp.tanh(half) + half).astype(BF16)
                    value = buf[pl.ds(g * size + o, keys), 2 * k + 1]
                    value = value.reshape(keys * block_len, head)
                    total += jnp.dot(weight, value, preferred_element_type=F32)
                total_ref[here, :] = total
                return 0

            lax.fori_loop(0, parts, one_part, 0)
            return 0

        lax.fori_loop(0, groups, one_group, 0)
        get_gate.wait()

        def finish(p, _):
            here = pl.ds(pl.multiple_of(p * part, part), part)
            total = total_ref[here, :]
            center = total - jnp.mean(total, axis=-1, keepdims=True)
            variance = jnp.mean(center * center, axis=-1, keepdims=True)
            scaled = center * lax.rsqrt(variance + 1e-05)
            out_ref[here, :] = (scaled * gate_ref[here, :]).astype(BF16)
            return 0

        def leave(p, _):
            here = pl.ds(pl.multiple_of(p * part, part), part)
            out_ref[here, :] = jnp.zeros((part, head), BF16)
            return 0

        lax.fori_loop(0, parts, finish, 0)
        lax.fori_loop(parts, rows // part, leave, 0)

    hbm = pl.BlockSpec(memory_space=pl.ANY)
    keys_all = owners * block_len * fields // 2
    return pl.pallas_call(
        body,
        out_shape=jax.ShapeDtypeStruct((rows, head), BF16),
        in_specs=[pl.BlockSpec(memory_space=pltpu.SMEM), hbm, hbm, hbm],
        out_specs=pl.BlockSpec(memory_space=pltpu.VMEM),
        scratch_shapes=[
            pltpu.VMEM((rows, head), BF16),
            pltpu.VMEM((rows, head), F32),
            pltpu.VMEM(history.shape, BF16),
            pltpu.VMEM((rows, head), F32),
            pltpu.SemaphoreType.DMA((groups,)),
            pltpu.SemaphoreType.DMA((2,)),
        ],
        compiler_params=pltpu.CompilerParams(vmem_limit_bytes=MOST_VMEM),
        cost_estimate=pl.CostEstimate(
            flops=4 * rows * keys_all * head,
            bytes_accessed=4 << 20,
            transcendentals=rows * keys_all,
        ),
        name="attend",
    )(count, query, gate, history)


def output_near(place, cand_rows, blocks, w_mine):
    n = lax.axis_size("mp")
    rows, width = blocks[0].shape
    tile = rows // 4
    steps = offsets(n)[: len(blocks)]

    def body(*refs):
        place_ref, rows_ref, w_ref = refs[:3]
        block_refs, out_ref = refs[3:-1], refs[-1]
        weights = [w_ref[columns(place_ref, s, n, width), :] for s in steps]
        for t in range(rows // tile):
            here = pl.ds(t * tile, tile)
            total = rows_ref[here, :].astype(F32)
            for ref, w in zip(block_refs, weights):
                total += jnp.dot(ref[here, :], w, preferred_element_type=F32)
            out_ref[here, :] = total

    vmem = pl.BlockSpec(memory_space=pltpu.VMEM)
    smem = pl.BlockSpec(memory_space=pltpu.SMEM)
    return pl.pallas_call(
        body,
        out_shape=jax.ShapeDtypeStruct((rows, width), F32),
        in_specs=[smem] + [vmem] * (2 + len(blocks)),
        out_specs=vmem,
        compiler_params=pltpu.CompilerParams(vmem_limit_bytes=VMEM),
        cost_estimate=pl.CostEstimate(
            flops=2 * rows * len(blocks) * width * width, bytes_accessed=2 << 20, transcendentals=0
        ),
        name="output_near",
    )(place, cand_rows, w_mine, *blocks)


def output(rows_all, place, count, near, blocks, top, bottom, w_mine):
    n = lax.axis_size("mp")
    rows, width = near.shape
    tile = rows // 4
    steps = offsets(n)[-1 - len(blocks) :]

    def body(*refs):
        place_ref, count_ref, near_ref, w_ref = refs[:4]
        block_refs = refs[4:-3]
        top_ref, bottom_ref, out_ref = refs[-3:]
        weights = [w_ref[columns(place_ref, s, n, width), :] for s in steps]
        for t in range(rows // tile):
            here = pl.ds(t * tile, tile)
            total = near_ref[here, :]
            for ref, w in zip(block_refs, weights):
                total += jnp.dot(ref[here, :], w, preferred_element_type=F32)
            far = top_ref if t * tile < rows // 2 else bottom_ref
            last = far[pl.ds((t * tile) % (rows // 2), tile), :]
            total += jnp.dot(last, weights[-1], preferred_element_type=F32)
            index = lax.broadcasted_iota(jnp.int32, (tile, width), 0) + t * tile
            out_ref[here, :] = jnp.where(index < count_ref[0], total, 0.0).astype(BF16)
        if rows < rows_all:
            out_ref[rows:, :] = jnp.zeros((rows_all - rows, width), BF16)

    vmem = pl.BlockSpec(memory_space=pltpu.VMEM)
    smem = pl.BlockSpec(memory_space=pltpu.SMEM)
    return pl.pallas_call(
        body,
        out_shape=jax.ShapeDtypeStruct((rows_all, width), BF16),
        in_specs=[smem, smem] + [vmem] * (4 + len(blocks)),
        out_specs=vmem,
        compiler_params=pltpu.CompilerParams(vmem_limit_bytes=VMEM),
        cost_estimate=pl.CostEstimate(
            flops=2 * rows * (len(blocks) + 1) * width * width,
            bytes_accessed=2 << 20,
            transcendentals=0,
        ),
        name="output",
    )(place, count, near, w_mine, *blocks, top, bottom)


def per_device(cand_rows, w_in, w_out, kv_pool, send_list, block_live, cand_count):
    head = kv_pool.shape[3]
    w_out = w_out.reshape(-1, w_out.shape[2])
    w_in = w_in.reshape(w_in.shape[0], -1)
    place = lax.axis_index("mp").astype(jnp.int32).reshape(1)
    packed = pack_live(send_list, block_live, kv_pool)
    history = lax.all_to_all(packed, "cache", split_axis=0, concat_axis=0, tiled=True)

    cand_later, _ = lax.optimization_barrier((cand_rows, packed))
    ups, downs = feature_rings(place, cand_later, w_out)
    gate, query, w_mine = project(
        place, cand_rows, w_out, ups, downs, w_in, 0.5 * head ** (-0.5)
    )

    def rest(rows):
        def run(gated, w_mine):
            heads, top, bottom = ring_gather(gated[:rows], "mp")
            near = output_near(place, cand_rows, heads[:-2], w_mine)
            total = cand_rows.shape[0]
            return output(total, place, cand_count, near, heads[-2:], top, bottom, w_mine)

        return run

    gated = attend(cand_count, query, gate, history)
    most = cand_rows.shape[0]
    return lax.cond(cand_count[0] <= most // 2, rest(most // 2), rest(most), gated, w_mine)


def solution(mesh):
    return jax.shard_map(
        per_device,
        mesh=mesh,
        in_specs=(
            P("cache", "mp"),
            P(None, "mp", None),
            P("mp", None, None),
            P(None, "cache", None, "mp"),
            P("cache", None),
            P("cache", None),
            P("cache"),
        ),
        out_specs=P("cache", "mp"),
        check_vma=False,
    )
```

```python
import jax
import jax.numpy as jnp
from jax import lax
from jax.experimental import pallas as pl
from jax.experimental.pallas import tpu as pltpu
from jax.sharding import PartitionSpec as P

BF16 = jnp.bfloat16
F32 = jnp.float32
VMEM = 16 * 1024 * 1024
MOST_VMEM = 60 * 1024 * 1024
LIVE = 2


def pack_live(send_list, block_live, kv_pool):
    pool = kv_pool.shape[1]
    tile = kv_pool.shape[2:]
    rankers = lax.axis_size("cache")
    slots = pool // rankers

    def body(send_hbm, live_hbm, pool_ref, out_ref, send_ref, live_ref, count_ref, buf, list_sem, in_sem, out_sem):
        lists = [
            pltpu.make_async_copy(send_hbm, send_ref, list_sem.at[0]),
            pltpu.make_async_copy(live_hbm, live_ref, list_sem.at[1]),
        ]
        for copy in lists:
            copy.start()
        for copy in lists:
            copy.wait()

        def fetch(r, _):
            at = [r * slots + s for s in range(slots)]
            first = last = send_ref[0, at[0]]
            count = live_ref[0, at[0]]
            for i in at[1:]:
                live = live_ref[0, i]
                block = send_ref[0, i]
                first = jnp.where(count > 0, first, block)
                last = jnp.where(live > 0, block, last)
                count = count + live
            count_ref[r] = count
            for k, block in enumerate((first, last)):
                there = buf.at[r, pl.ds(2 * k, 2)]
                pltpu.make_async_copy(pool_ref.at[:, block], there, in_sem.at[r]).start(priority=k)
            return 0

        def pass_on(r, _):
            pltpu.make_async_copy(buf.at[r], buf.at[r], in_sem.at[r]).wait()
            for k in range(LIVE):

                @pl.when(count_ref[r] <= k)
                def _():
                    buf[r, pl.ds(2 * k, 2)] = jnp.zeros((2,) + tile, BF16)

            pltpu.make_async_copy(buf.at[r], out_ref.at[r], out_sem).start()
            return 0

        lax.fori_loop(0, rankers, fetch, 0, unroll=8)
        lax.fori_loop(0, rankers, pass_on, 0, unroll=4)
        pltpu.make_async_copy(buf, out_ref, out_sem).wait()

    hbm = pl.BlockSpec(memory_space=pl.ANY)
    return pl.pallas_call(
        body,
        out_shape=jax.ShapeDtypeStruct((rankers, 2 * LIVE) + tile, BF16),
        in_specs=[hbm, hbm, hbm],
        out_specs=hbm,
        scratch_shapes=[
            pltpu.SMEM(send_list.shape, jnp.int32),
            pltpu.SMEM(block_live.shape, jnp.int32),
            pltpu.SMEM((rankers,), jnp.int32),
            pltpu.VMEM((rankers, 2 * LIVE) + tile, BF16),
            pltpu.SemaphoreType.DMA((2,)),
            pltpu.SemaphoreType.DMA((rankers,)),
            pltpu.SemaphoreType.DMA,
        ],
        compiler_params=pltpu.CompilerParams(vmem_limit_bytes=MOST_VMEM),
        name="pack_live",
    )(send_list, block_live, kv_pool)


def stage(place, cand_rows, w_out):
    n = lax.axis_size("mp")
    rows, width = cand_rows.shape
    depth = w_out.shape[0]
    half = depth // 2
    total = rows + half + (n // 2 - 1) * depth

    def body(place_ref, rows_ref, w_ref, up_ref, down_ref, sem):
        def weights(k):
            start = pl.multiple_of(lax.rem(place_ref[0] + (k + n), n) * width, width)
            return w_ref.at[:, pl.ds(start, width)]

        copies = [
            (rows_ref, up_ref.at[pl.ds(half, rows)]),
            (rows_ref, down_ref.at[pl.ds(0, rows)]),
            (weights(n // 2).at[pl.ds(0, half)], up_ref.at[pl.ds(0, half)]),
            (weights(n // 2).at[pl.ds(half, half)], down_ref.at[pl.ds(rows, half)]),
        ]
        for k in range(1, n // 2):
            at = pl.ds(total - k * depth, depth)
            copies += [(weights(k), up_ref.at[at]), (weights(-k), down_ref.at[at])]
        copies = [pltpu.make_async_copy(a, b, sem.at[i]) for i, (a, b) in enumerate(copies)]
        for copy in copies:
            copy.start()
        for copy in copies:
            copy.wait()

    hbm = pl.BlockSpec(memory_space=pltpu.HBM)
    vmem = pl.BlockSpec(memory_space=pltpu.VMEM)
    shape = jax.ShapeDtypeStruct((total, width), BF16)
    return pl.pallas_call(
        body,
        out_shape=(shape, shape),
        in_specs=[pl.BlockSpec(memory_space=pltpu.SMEM), hbm, hbm],
        out_specs=(vmem, vmem),
        scratch_shapes=[pltpu.SemaphoreType.DMA((n + 2,))],
        compiler_params=pltpu.CompilerParams(vmem_limit_bytes=VMEM),
        name="stage",
    )(place, cand_rows, w_out)


def feature_rings(place, cand_rows, w_out):
    n = lax.axis_size("mp")
    rows = cand_rows.shape[0]
    depth = w_out.shape[0]
    half = depth // 2
    up = [(i, (i + 1) % n) for i in range(n)]
    down = [(i, (i - 1) % n) for i in range(n)]
    a, b = stage(place, cand_rows, w_out)
    ups, downs = [], []
    for k in range(n // 2 - 1):
        a = lax.ppermute(a, "mp", up)
        b = lax.ppermute(b, "mp", down)
        ups.append(a)
        downs.append(b)
        if k < n // 2 - 2:
            a, b = a[:-depth], b[:-depth]
    a = lax.ppermute(a[: half + rows // 2], "mp", up)
    b = lax.ppermute(b[rows // 2 : rows + half], "mp", down)
    return ups + [a], downs + [b]


def ring_gather(x, axis):
    n = lax.axis_size(axis)
    up = [(i, (i + 1) % n) for i in range(n)]
    down = [(i, (i - 1) % n) for i in range(n)]
    got = [x]
    left = right = x
    for _ in range(n // 2 - 1):
        left = lax.ppermute(left, axis, up)
        right = lax.ppermute(right, axis, down)
        got += [right, left]
    half = x.shape[0] // 2
    top = lax.ppermute(left[:half], axis, up)
    bottom = lax.ppermute(right[half:], axis, down)
    return got, top, bottom


def columns(place_ref, distance, n, width):
    start = lax.rem(place_ref[0] + (distance + n), n) * width
    return pl.ds(pl.multiple_of(start, width), width)


def offsets(n):
    order = [0]
    for s in range(1, n // 2):
        order += [s, -s]
    return order + [n // 2]


def project(place, cand_rows, w_out, ups, downs, w_in, scale):
    n = lax.axis_size("mp")
    rows, width = cand_rows.shape
    depth = w_out.shape[0]
    half = depth // 2
    cols = w_in.shape[1]
    tile = rows // 4
    far = n // 2

    def body(*refs):
        place_ref, rows_ref, w_out_ref, w_in_hbm = refs[:4]
        up_refs, down_refs = refs[4 : 4 + far], refs[4 + far : 4 + 2 * far]
        gate_ref, query_ref, w_mine_ref, x_ref, w_in_ref, sem = refs[4 + 2 * far :]

        def spot(k):
            return lax.rem(place_ref[0] + (k + n), n)

        def columns(k):
            return pl.ds(pl.multiple_of(spot(k) * width, width), width)

        def weight_rows(k, start, size):
            return w_mine_ref.at[pl.ds(pl.multiple_of(spot(k) * depth + start, half), size)]

        copies = [
            (w_in_hbm, w_in_ref),
            (rows_ref, x_ref.at[:, columns(0)]),
            (w_out_ref.at[:, columns(0)], weight_rows(0, 0, depth)),
        ]
        for k in range(1, far):
            last = pl.ds(rows + half + (far - 1 - k) * depth, depth)
            copies += [
                (up_refs[k - 1].at[pl.ds(half, rows)], x_ref.at[:, columns(-k)]),
                (up_refs[k - 1].at[last], weight_rows(-k, 0, depth)),
                (down_refs[k - 1].at[pl.ds(0, rows)], x_ref.at[:, columns(k)]),
                (down_refs[k - 1].at[last], weight_rows(k, 0, depth)),
            ]
        top, bottom = pl.ds(0, rows // 2), pl.ds(rows // 2, rows // 2)
        copies += [
            (up_refs[-1].at[pl.ds(half, rows // 2)], x_ref.at[top, columns(far)]),
            (up_refs[-1].at[pl.ds(0, half)], weight_rows(far, 0, half)),
            (down_refs[-1].at[pl.ds(0, rows // 2)], x_ref.at[bottom, columns(far)]),
            (down_refs[-1].at[pl.ds(rows // 2, half)], weight_rows(far, half, half)),
        ]
        copies = [pltpu.make_async_copy(a, b, sem.at[i]) for i, (a, b) in enumerate(copies)]
        for copy in copies:
            copy.start()
        for copy in copies:
            copy.wait()
        for t in range(rows // tile):
            here = pl.ds(t * tile, tile)
            total = jnp.dot(x_ref[here, :], w_in_ref[...], preferred_element_type=F32)
            gate = total[:, : cols // 2]
            query = total[:, cols // 2 :]
            gate_ref[here, :] = gate / (1.0 + jnp.exp(-gate))
            query_ref[here, :] = (query / (1.0 + jnp.exp(-query)) * scale).astype(BF16)

    vmem = pl.BlockSpec(memory_space=pltpu.VMEM)
    hbm = pl.BlockSpec(memory_space=pltpu.HBM)
    return pl.pallas_call(
        body,
        out_shape=(
            jax.ShapeDtypeStruct((rows, cols // 2), F32),
            jax.ShapeDtypeStruct((rows, cols // 2), BF16),
            jax.ShapeDtypeStruct((n * depth, width), BF16),
        ),
        in_specs=[pl.BlockSpec(memory_space=pltpu.SMEM)] + [hbm] * (3 + 2 * far),
        out_specs=(vmem, vmem, vmem),
        scratch_shapes=[
            pltpu.VMEM((rows, n * width), BF16),
            pltpu.VMEM(w_in.shape, BF16),
            pltpu.SemaphoreType.DMA((3 + 4 * far,)),
        ],
        compiler_params=pltpu.CompilerParams(vmem_limit_bytes=VMEM),
        cost_estimate=pl.CostEstimate(
            flops=2 * rows * n * width * cols, bytes_accessed=4 << 20, transcendentals=rows * cols
        ),
        name="project",
    )(place, cand_rows, w_out, w_in, *ups, *downs)


def attend(count, query, gate, history):
    rows, head = query.shape
    owners, fields, block_len, _ = history.shape
    keys = 4
    groups = [(0, owners // 4), (owners // 4, owners - owners // 4)]
    part = rows // 2

    def body(count_ref, query_hbm, gate_hbm, history_hbm, out_ref, query_ref, gate_ref, buf, total_ref, sem, own_sem):
        get_query = pltpu.make_async_copy(query_hbm, query_ref, own_sem.at[0])
        get_gate = pltpu.make_async_copy(gate_hbm, gate_ref, own_sem.at[1])
        get_query.start()

        copies = []
        for i, (start, size) in enumerate(groups):
            here = pl.ds(start, size)
            copies.append(pltpu.make_async_copy(history_hbm.at[here], buf.at[here], sem.at[i]))
        for copy in copies:
            copy.start()
        get_gate.start()
        total_ref[...] = jnp.zeros_like(total_ref)
        get_query.wait()
        parts = lax.div(count_ref[0] + (part - 1), part)

        def one_group(start, size):
            def one_part(p, _):
                here = pl.ds(pl.multiple_of(p * part, part), part)
                query = query_ref[here, :]
                total = total_ref[here, :]

                def score(unit):
                    k, o = unit
                    key = buf[o : o + keys, 2 * k].reshape(keys * block_len, head)
                    return lax.dot_general(
                        query, key, (((1,), (1,)), ((), ())), preferred_element_type=F32
                    )

                units = [(k, o) for o in range(start, start + size, keys) for k in range(fields // 2)]
                ahead = score(units[0])
                for i, (k, o) in enumerate(units):
                    half = ahead
                    if i + 1 < len(units):
                        ahead = score(units[i + 1])
                    weight = (half * jnp.tanh(half) + half).astype(BF16)
                    value = buf[o : o + keys, 2 * k + 1]
                    value = value.reshape(keys * block_len, head)
                    total += jnp.dot(weight, value, preferred_element_type=F32)
                total_ref[here, :] = total
                return 0

            lax.fori_loop(0, parts, one_part, 0)

        for copy, (start, size) in zip(copies, groups):
            copy.wait()
            one_group(start, size)
        get_gate.wait()

        def finish(p, _):
            here = pl.ds(pl.multiple_of(p * part, part), part)
            total = total_ref[here, :]
            center = total - jnp.mean(total, axis=-1, keepdims=True)
            variance = jnp.mean(center * center, axis=-1, keepdims=True)
            scaled = center * lax.rsqrt(variance + 1e-05)
            out_ref[here, :] = (scaled * gate_ref[here, :]).astype(BF16)
            return 0

        def leave(p, _):
            here = pl.ds(pl.multiple_of(p * part, part), part)
            out_ref[here, :] = jnp.zeros((part, head), BF16)
            return 0

        lax.fori_loop(0, parts, finish, 0)
        lax.fori_loop(parts, rows // part, leave, 0)

    hbm = pl.BlockSpec(memory_space=pl.ANY)
    keys_all = owners * block_len * fields // 2
    return pl.pallas_call(
        body,
        out_shape=jax.ShapeDtypeStruct((rows, head), BF16),
        in_specs=[pl.BlockSpec(memory_space=pltpu.SMEM), hbm, hbm, hbm],
        out_specs=pl.BlockSpec(memory_space=pltpu.VMEM),
        scratch_shapes=[
            pltpu.VMEM((rows, head), BF16),
            pltpu.VMEM((rows, head), F32),
            pltpu.VMEM(history.shape, BF16),
            pltpu.VMEM((rows, head), F32),
            pltpu.SemaphoreType.DMA((len(groups),)),
            pltpu.SemaphoreType.DMA((2,)),
        ],
        compiler_params=pltpu.CompilerParams(vmem_limit_bytes=MOST_VMEM),
        cost_estimate=pl.CostEstimate(
            flops=4 * rows * keys_all * head,
            bytes_accessed=4 << 20,
            transcendentals=rows * keys_all,
        ),
        name="attend",
    )(count, query, gate, history)


def output_near(place, cand_rows, blocks, w_mine):
    n = lax.axis_size("mp")
    rows, width = blocks[0].shape
    tile = rows // 4
    steps = offsets(n)[: len(blocks)]

    def body(*refs):
        place_ref, rows_ref, w_ref = refs[:3]
        block_refs, out_ref = refs[3:-1], refs[-1]
        weights = [w_ref[columns(place_ref, s, n, width), :] for s in steps]
        for t in range(rows // tile):
            here = pl.ds(t * tile, tile)
            total = rows_ref[here, :].astype(F32)
            for ref, w in zip(block_refs, weights):
                total += jnp.dot(ref[here, :], w, preferred_element_type=F32)
            out_ref[here, :] = total

    vmem = pl.BlockSpec(memory_space=pltpu.VMEM)
    smem = pl.BlockSpec(memory_space=pltpu.SMEM)
    return pl.pallas_call(
        body,
        out_shape=jax.ShapeDtypeStruct((rows, width), F32),
        in_specs=[smem] + [vmem] * (2 + len(blocks)),
        out_specs=vmem,
        compiler_params=pltpu.CompilerParams(vmem_limit_bytes=VMEM),
        cost_estimate=pl.CostEstimate(
            flops=2 * rows * len(blocks) * width * width, bytes_accessed=2 << 20, transcendentals=0
        ),
        name="output_near",
    )(place, cand_rows, w_mine, *blocks)


def output(rows_all, place, count, near, blocks, top, bottom, w_mine):
    n = lax.axis_size("mp")
    rows, width = near.shape
    tile = rows // 4
    steps = offsets(n)[-1 - len(blocks) :]

    def body(*refs):
        place_ref, count_ref, near_ref, w_ref = refs[:4]
        block_refs = refs[4:-3]
        top_ref, bottom_ref, out_ref = refs[-3:]
        weights = [w_ref[columns(place_ref, s, n, width), :] for s in steps]
        for t in range(rows // tile):
            here = pl.ds(t * tile, tile)
            total = near_ref[here, :]
            for ref, w in zip(block_refs, weights):
                total += jnp.dot(ref[here, :], w, preferred_element_type=F32)
            far = top_ref if t * tile < rows // 2 else bottom_ref
            last = far[pl.ds((t * tile) % (rows // 2), tile), :]
            total += jnp.dot(last, weights[-1], preferred_element_type=F32)
            index = lax.broadcasted_iota(jnp.int32, (tile, width), 0) + t * tile
            out_ref[here, :] = jnp.where(index < count_ref[0], total, 0.0).astype(BF16)
        if rows < rows_all:
            out_ref[rows:, :] = jnp.zeros((rows_all - rows, width), BF16)

    vmem = pl.BlockSpec(memory_space=pltpu.VMEM)
    smem = pl.BlockSpec(memory_space=pltpu.SMEM)
    return pl.pallas_call(
        body,
        out_shape=jax.ShapeDtypeStruct((rows_all, width), BF16),
        in_specs=[smem, smem] + [vmem] * (4 + len(blocks)),
        out_specs=vmem,
        compiler_params=pltpu.CompilerParams(vmem_limit_bytes=VMEM),
        cost_estimate=pl.CostEstimate(
            flops=2 * rows * (len(blocks) + 1) * width * width,
            bytes_accessed=2 << 20,
            transcendentals=0,
        ),
        name="output",
    )(place, count, near, w_mine, *blocks, top, bottom)


def per_device(cand_rows, w_in, w_out, kv_pool, send_list, block_live, cand_count):
    head = kv_pool.shape[3]
    w_out = w_out.reshape(-1, w_out.shape[2])
    w_in = w_in.reshape(w_in.shape[0], -1)
    place = lax.axis_index("mp").astype(jnp.int32).reshape(1)
    packed = pack_live(send_list, block_live, kv_pool)
    history = lax.all_to_all(packed, "cache", split_axis=0, concat_axis=0, tiled=True)

    cand_later, _ = lax.optimization_barrier((cand_rows, packed))
    ups, downs = feature_rings(place, cand_later, w_out)
    gate, query, w_mine = project(
        place, cand_rows, w_out, ups, downs, w_in, 0.5 * head ** (-0.5)
    )

    def rest(rows):
        def run(gated, w_mine):
            heads, top, bottom = ring_gather(gated[:rows], "mp")
            near = output_near(place, cand_rows, heads[:-2], w_mine)
            total = cand_rows.shape[0]
            return output(total, place, cand_count, near, heads[-2:], top, bottom, w_mine)

        return run

    gated = attend(cand_count, query, gate, history)
    most = cand_rows.shape[0]
    return lax.cond(cand_count[0] <= most // 2, rest(most // 2), rest(most), gated, w_mine)


def solution(mesh):
    return jax.shard_map(
        per_device,
        mesh=mesh,
        in_specs=(
            P("cache", "mp"),
            P(None, "mp", None),
            P("mp", None, None),
            P(None, "cache", None, "mp"),
            P("cache", None),
            P("cache", None),
            P("cache"),
        ),
        out_specs=P("cache", "mp"),
        check_vma=False,
    )
```

```python
import jax
import jax.numpy as jnp
from jax import lax
from jax.experimental import pallas as pl
from jax.experimental.pallas import tpu as pltpu
from jax.sharding import PartitionSpec as P

BF16 = jnp.bfloat16
F32 = jnp.float32
VMEM = 16 * 1024 * 1024
MOST_VMEM = 60 * 1024 * 1024
LIVE = 2


def pack_live(send_list, block_live, kv_pool):
    pool = kv_pool.shape[1]
    tile = kv_pool.shape[2:]
    rankers = lax.axis_size("cache")
    slots = pool // rankers

    def body(send_hbm, live_hbm, pool_ref, out_ref, send_ref, live_ref, count_ref, buf, list_sem, in_sem, out_sem):
        lists = [
            pltpu.make_async_copy(send_hbm, send_ref, list_sem.at[0]),
            pltpu.make_async_copy(live_hbm, live_ref, list_sem.at[1]),
        ]
        for queue, copy in enumerate(lists):
            copy.start(priority=queue)
        for copy in lists:
            copy.wait()

        def fetch(r, _):
            at = [r * slots + s for s in range(slots)]
            first = last = send_ref[0, at[0]]
            count = live_ref[0, at[0]]
            for i in at[1:]:
                live = live_ref[0, i]
                block = send_ref[0, i]
                first = jnp.where(count > 0, first, block)
                last = jnp.where(live > 0, block, last)
                count = count + live
            count_ref[r] = count
            for k, block in enumerate((first, last)):
                there = buf.at[r, pl.ds(2 * k, 2)]
                pltpu.make_async_copy(pool_ref.at[:, block], there, in_sem.at[r]).start(priority=k)
            return 0

        def pass_on(r, _):
            pltpu.make_async_copy(buf.at[r], buf.at[r], in_sem.at[r]).wait()
            for k in range(LIVE):

                @pl.when(count_ref[r] <= k)
                def _():
                    buf[r, pl.ds(2 * k, 2)] = jnp.zeros((2,) + tile, BF16)

            pltpu.make_async_copy(buf.at[r], out_ref.at[r], out_sem).start()
            return 0

        lax.fori_loop(0, rankers, fetch, 0, unroll=8)
        lax.fori_loop(0, rankers, pass_on, 0, unroll=4)
        pltpu.make_async_copy(buf, out_ref, out_sem).wait()

    hbm = pl.BlockSpec(memory_space=pl.ANY)
    return pl.pallas_call(
        body,
        out_shape=jax.ShapeDtypeStruct((rankers, 2 * LIVE) + tile, BF16),
        in_specs=[hbm, hbm, hbm],
        out_specs=hbm,
        scratch_shapes=[
            pltpu.SMEM(send_list.shape, jnp.int32),
            pltpu.SMEM(block_live.shape, jnp.int32),
            pltpu.SMEM((rankers,), jnp.int32),
            pltpu.VMEM((rankers, 2 * LIVE) + tile, BF16),
            pltpu.SemaphoreType.DMA((2,)),
            pltpu.SemaphoreType.DMA((rankers,)),
            pltpu.SemaphoreType.DMA,
        ],
        compiler_params=pltpu.CompilerParams(vmem_limit_bytes=MOST_VMEM),
        name="pack_live",
    )(send_list, block_live, kv_pool)


def stage(place, cand_rows, w_out):
    n = lax.axis_size("mp")
    rows, width = cand_rows.shape
    depth = w_out.shape[0]
    half = depth // 2
    total = rows + half + (n // 2 - 1) * depth

    def body(place_ref, rows_ref, w_ref, up_ref, down_ref, sem):
        def weights(k):
            start = pl.multiple_of(lax.rem(place_ref[0] + (k + n), n) * width, width)
            return w_ref.at[:, pl.ds(start, width)]

        copies = [
            (rows_ref, up_ref.at[pl.ds(half, rows)]),
            (rows_ref, down_ref.at[pl.ds(0, rows)]),
            (weights(n // 2).at[pl.ds(0, half)], up_ref.at[pl.ds(0, half)]),
            (weights(n // 2).at[pl.ds(half, half)], down_ref.at[pl.ds(rows, half)]),
        ]
        for k in range(1, n // 2):
            at = pl.ds(total - k * depth, depth)
            copies += [(weights(k), up_ref.at[at]), (weights(-k), down_ref.at[at])]
        copies = [pltpu.make_async_copy(a, b, sem.at[i]) for i, (a, b) in enumerate(copies)]
        for copy in copies:
            copy.start()
        for copy in copies:
            copy.wait()

    hbm = pl.BlockSpec(memory_space=pltpu.HBM)
    vmem = pl.BlockSpec(memory_space=pltpu.VMEM)
    shape = jax.ShapeDtypeStruct((total, width), BF16)
    return pl.pallas_call(
        body,
        out_shape=(shape, shape),
        in_specs=[pl.BlockSpec(memory_space=pltpu.SMEM), hbm, hbm],
        out_specs=(vmem, vmem),
        scratch_shapes=[pltpu.SemaphoreType.DMA((n + 2,))],
        compiler_params=pltpu.CompilerParams(vmem_limit_bytes=VMEM),
        name="stage",
    )(place, cand_rows, w_out)


def feature_rings(place, cand_rows, w_out):
    n = lax.axis_size("mp")
    rows = cand_rows.shape[0]
    depth = w_out.shape[0]
    half = depth // 2
    up = [(i, (i + 1) % n) for i in range(n)]
    down = [(i, (i - 1) % n) for i in range(n)]
    a, b = stage(place, cand_rows, w_out)
    ups, downs = [], []
    for k in range(n // 2 - 1):
        a = lax.ppermute(a, "mp", up)
        b = lax.ppermute(b, "mp", down)
        ups.append(a)
        downs.append(b)
        if k < n // 2 - 2:
            a, b = a[:-depth], b[:-depth]
    a = lax.ppermute(a[: half + rows // 2], "mp", up)
    b = lax.ppermute(b[rows // 2 : rows + half], "mp", down)
    return ups + [a], downs + [b]


def ring_gather(x, axis):
    n = lax.axis_size(axis)
    up = [(i, (i + 1) % n) for i in range(n)]
    down = [(i, (i - 1) % n) for i in range(n)]
    got = [x]
    left = right = x
    for _ in range(n // 2 - 1):
        left = lax.ppermute(left, axis, up)
        right = lax.ppermute(right, axis, down)
        got += [right, left]
    half = x.shape[0] // 2
    top = lax.ppermute(left[:half], axis, up)
    bottom = lax.ppermute(right[half:], axis, down)
    return got, top, bottom


def columns(place_ref, distance, n, width):
    start = lax.rem(place_ref[0] + (distance + n), n) * width
    return pl.ds(pl.multiple_of(start, width), width)


def offsets(n):
    order = [0]
    for s in range(1, n // 2):
        order += [s, -s]
    return order + [n // 2]


def project(place, cand_rows, w_out, ups, downs, w_in, scale):
    n = lax.axis_size("mp")
    rows, width = cand_rows.shape
    depth = w_out.shape[0]
    half = depth // 2
    cols = w_in.shape[1]
    tile = rows // 4
    far = n // 2

    def body(*refs):
        place_ref, rows_ref, w_out_ref, w_in_hbm = refs[:4]
        up_refs, down_refs = refs[4 : 4 + far], refs[4 + far : 4 + 2 * far]
        gate_ref, query_ref, w_mine_ref, x_ref, w_in_ref, sem = refs[4 + 2 * far :]

        def spot(k):
            return lax.rem(place_ref[0] + (k + n), n)

        def columns(k):
            return pl.ds(pl.multiple_of(spot(k) * width, width), width)

        def weight_rows(k, start, size):
            return w_mine_ref.at[pl.ds(pl.multiple_of(spot(k) * depth + start, half), size)]

        copies = [
            (w_in_hbm, w_in_ref),
            (rows_ref, x_ref.at[:, columns(0)]),
            (w_out_ref.at[:, columns(0)], weight_rows(0, 0, depth)),
        ]
        for k in range(1, far):
            last = pl.ds(rows + half + (far - 1 - k) * depth, depth)
            copies += [
                (up_refs[k - 1].at[pl.ds(half, rows)], x_ref.at[:, columns(-k)]),
                (up_refs[k - 1].at[last], weight_rows(-k, 0, depth)),
                (down_refs[k - 1].at[pl.ds(0, rows)], x_ref.at[:, columns(k)]),
                (down_refs[k - 1].at[last], weight_rows(k, 0, depth)),
            ]
        top, bottom = pl.ds(0, rows // 2), pl.ds(rows // 2, rows // 2)
        copies += [
            (up_refs[-1].at[pl.ds(half, rows // 2)], x_ref.at[top, columns(far)]),
            (up_refs[-1].at[pl.ds(0, half)], weight_rows(far, 0, half)),
            (down_refs[-1].at[pl.ds(0, rows // 2)], x_ref.at[bottom, columns(far)]),
            (down_refs[-1].at[pl.ds(rows // 2, half)], weight_rows(far, half, half)),
        ]
        copies = [pltpu.make_async_copy(a, b, sem.at[i]) for i, (a, b) in enumerate(copies)]
        for copy in copies:
            copy.start()
        for copy in copies:
            copy.wait()
        for t in range(rows // tile):
            here = pl.ds(t * tile, tile)
            total = jnp.dot(x_ref[here, :], w_in_ref[...], preferred_element_type=F32)
            gate = total[:, : cols // 2]
            query = total[:, cols // 2 :]
            gate_ref[here, :] = gate / (1.0 + jnp.exp(-gate))
            query_ref[here, :] = (query / (1.0 + jnp.exp(-query)) * scale).astype(BF16)

    vmem = pl.BlockSpec(memory_space=pltpu.VMEM)
    hbm = pl.BlockSpec(memory_space=pltpu.HBM)
    return pl.pallas_call(
        body,
        out_shape=(
            jax.ShapeDtypeStruct((rows, cols // 2), F32),
            jax.ShapeDtypeStruct((rows, cols // 2), BF16),
            jax.ShapeDtypeStruct((n * depth, width), BF16),
        ),
        in_specs=[pl.BlockSpec(memory_space=pltpu.SMEM)] + [hbm] * (3 + 2 * far),
        out_specs=(vmem, vmem, vmem),
        scratch_shapes=[
            pltpu.VMEM((rows, n * width), BF16),
            pltpu.VMEM(w_in.shape, BF16),
            pltpu.SemaphoreType.DMA((3 + 4 * far,)),
        ],
        compiler_params=pltpu.CompilerParams(vmem_limit_bytes=VMEM),
        cost_estimate=pl.CostEstimate(
            flops=2 * rows * n * width * cols, bytes_accessed=4 << 20, transcendentals=rows * cols
        ),
        name="project",
    )(place, cand_rows, w_out, w_in, *ups, *downs)


def attend(count, query, gate, history):
    rows, head = query.shape
    owners, fields, block_len, _ = history.shape
    keys = 4
    groups = [(0, owners // 4), (owners // 4, owners - owners // 4)]
    part = rows // 2

    def body(count_ref, query_hbm, gate_hbm, history_hbm, out_ref, query_ref, gate_ref, buf, total_ref, sem, own_sem):
        get_query = pltpu.make_async_copy(query_hbm, query_ref, own_sem.at[0])
        get_gate = pltpu.make_async_copy(gate_hbm, gate_ref, own_sem.at[1])
        get_query.start(priority=1)

        copies = []
        for i, (start, size) in enumerate(groups):
            here = pl.ds(start, size)
            copies.append(pltpu.make_async_copy(history_hbm.at[here], buf.at[here], sem.at[i]))
        for copy in copies:
            copy.start()
        get_gate.start(priority=1)
        total_ref[...] = jnp.zeros_like(total_ref)
        get_query.wait()
        parts = lax.div(count_ref[0] + (part - 1), part)

        def one_group(start, size):
            def one_part(p, _):
                here = pl.ds(pl.multiple_of(p * part, part), part)
                query = query_ref[here, :]
                total = total_ref[here, :]

                def score(unit):
                    k, o = unit
                    key = buf[o : o + keys, 2 * k].reshape(keys * block_len, head)
                    return lax.dot_general(
                        query, key, (((1,), (1,)), ((), ())), preferred_element_type=F32
                    )

                units = [(k, o) for o in range(start, start + size, keys) for k in range(fields // 2)]
                ahead = score(units[0])
                for i, (k, o) in enumerate(units):
                    half = ahead
                    if i + 1 < len(units):
                        ahead = score(units[i + 1])
                    weight = (half * jnp.tanh(half) + half).astype(BF16)
                    value = buf[o : o + keys, 2 * k + 1]
                    value = value.reshape(keys * block_len, head)
                    total += jnp.dot(weight, value, preferred_element_type=F32)
                total_ref[here, :] = total
                return 0

            lax.fori_loop(0, parts, one_part, 0)

        for copy, (start, size) in zip(copies, groups):
            copy.wait()
            one_group(start, size)
        get_gate.wait()

        def finish(p, _):
            here = pl.ds(pl.multiple_of(p * part, part), part)
            total = total_ref[here, :]
            center = total - jnp.mean(total, axis=-1, keepdims=True)
            variance = jnp.mean(center * center, axis=-1, keepdims=True)
            scaled = center * lax.rsqrt(variance + 1e-05)
            out_ref[here, :] = (scaled * gate_ref[here, :]).astype(BF16)
            return 0

        def leave(p, _):
            here = pl.ds(pl.multiple_of(p * part, part), part)
            out_ref[here, :] = jnp.zeros((part, head), BF16)
            return 0

        lax.fori_loop(0, parts, finish, 0)
        lax.fori_loop(parts, rows // part, leave, 0)

    hbm = pl.BlockSpec(memory_space=pl.ANY)
    keys_all = owners * block_len * fields // 2
    return pl.pallas_call(
        body,
        out_shape=jax.ShapeDtypeStruct((rows, head), BF16),
        in_specs=[pl.BlockSpec(memory_space=pltpu.SMEM), hbm, hbm, hbm],
        out_specs=pl.BlockSpec(memory_space=pltpu.VMEM),
        scratch_shapes=[
            pltpu.VMEM((rows, head), BF16),
            pltpu.VMEM((rows, head), F32),
            pltpu.VMEM(history.shape, BF16),
            pltpu.VMEM((rows, head), F32),
            pltpu.SemaphoreType.DMA((len(groups),)),
            pltpu.SemaphoreType.DMA((2,)),
        ],
        compiler_params=pltpu.CompilerParams(vmem_limit_bytes=MOST_VMEM),
        cost_estimate=pl.CostEstimate(
            flops=4 * rows * keys_all * head,
            bytes_accessed=4 << 20,
            transcendentals=rows * keys_all,
        ),
        name="attend",
    )(count, query, gate, history)


def output_near(place, cand_rows, blocks, w_mine):
    n = lax.axis_size("mp")
    rows, width = blocks[0].shape
    tile = rows // 4
    steps = offsets(n)[: len(blocks)]

    def body(*refs):
        place_ref, rows_ref, w_ref = refs[:3]
        block_refs, out_ref = refs[3:-1], refs[-1]
        weights = [w_ref[columns(place_ref, s, n, width), :] for s in steps]
        for t in range(rows // tile):
            here = pl.ds(t * tile, tile)
            total = rows_ref[here, :].astype(F32)
            for ref, w in zip(block_refs, weights):
                total += jnp.dot(ref[here, :], w, preferred_element_type=F32)
            out_ref[here, :] = total

    vmem = pl.BlockSpec(memory_space=pltpu.VMEM)
    smem = pl.BlockSpec(memory_space=pltpu.SMEM)
    return pl.pallas_call(
        body,
        out_shape=jax.ShapeDtypeStruct((rows, width), F32),
        in_specs=[smem] + [vmem] * (2 + len(blocks)),
        out_specs=vmem,
        compiler_params=pltpu.CompilerParams(vmem_limit_bytes=VMEM),
        cost_estimate=pl.CostEstimate(
            flops=2 * rows * len(blocks) * width * width, bytes_accessed=2 << 20, transcendentals=0
        ),
        name="output_near",
    )(place, cand_rows, w_mine, *blocks)


def output(rows_all, place, count, near, blocks, top, bottom, w_mine):
    n = lax.axis_size("mp")
    rows, width = near.shape
    tile = rows // 4
    steps = offsets(n)[-1 - len(blocks) :]

    def body(*refs):
        place_ref, count_ref, near_ref, w_ref = refs[:4]
        block_refs = refs[4:-3]
        top_ref, bottom_ref, out_ref = refs[-3:]
        weights = [w_ref[columns(place_ref, s, n, width), :] for s in steps]
        for t in range(rows // tile):
            here = pl.ds(t * tile, tile)
            total = near_ref[here, :]
            for ref, w in zip(block_refs, weights):
                total += jnp.dot(ref[here, :], w, preferred_element_type=F32)
            far = top_ref if t * tile < rows // 2 else bottom_ref
            last = far[pl.ds((t * tile) % (rows // 2), tile), :]
            total += jnp.dot(last, weights[-1], preferred_element_type=F32)
            index = lax.broadcasted_iota(jnp.int32, (tile, width), 0) + t * tile
            out_ref[here, :] = jnp.where(index < count_ref[0], total, 0.0).astype(BF16)
        if rows < rows_all:
            out_ref[rows:, :] = jnp.zeros((rows_all - rows, width), BF16)

    vmem = pl.BlockSpec(memory_space=pltpu.VMEM)
    smem = pl.BlockSpec(memory_space=pltpu.SMEM)
    return pl.pallas_call(
        body,
        out_shape=jax.ShapeDtypeStruct((rows_all, width), BF16),
        in_specs=[smem, smem] + [vmem] * (4 + len(blocks)),
        out_specs=vmem,
        compiler_params=pltpu.CompilerParams(vmem_limit_bytes=VMEM),
        cost_estimate=pl.CostEstimate(
            flops=2 * rows * (len(blocks) + 1) * width * width,
            bytes_accessed=2 << 20,
            transcendentals=0,
        ),
        name="output",
    )(place, count, near, w_mine, *blocks, top, bottom)


def per_device(cand_rows, w_in, w_out, kv_pool, send_list, block_live, cand_count):
    head = kv_pool.shape[3]
    w_out = w_out.reshape(-1, w_out.shape[2])
    w_in = w_in.reshape(w_in.shape[0], -1)
    place = lax.axis_index("mp").astype(jnp.int32).reshape(1)
    packed = pack_live(send_list, block_live, kv_pool)
    history = lax.all_to_all(packed, "cache", split_axis=0, concat_axis=0, tiled=True)

    cand_later, _ = lax.optimization_barrier((cand_rows, packed))
    ups, downs = feature_rings(place, cand_later, w_out)
    gate, query, w_mine = project(
        place, cand_rows, w_out, ups, downs, w_in, 0.5 * head ** (-0.5)
    )

    def rest(rows):
        def run(gated, w_mine):
            heads, top, bottom = ring_gather(gated[:rows], "mp")
            near = output_near(place, cand_rows, heads[:-2], w_mine)
            total = cand_rows.shape[0]
            return output(total, place, cand_count, near, heads[-2:], top, bottom, w_mine)

        return run

    gated = attend(cand_count, query, gate, history)
    most = cand_rows.shape[0]
    return lax.cond(cand_count[0] <= most // 2, rest(most // 2), rest(most), gated, w_mine)


def solution(mesh):
    return jax.shard_map(
        per_device,
        mesh=mesh,
        in_specs=(
            P("cache", "mp"),
            P(None, "mp", None),
            P("mp", None, None),
            P(None, "cache", None, "mp"),
            P("cache", None),
            P("cache", None),
            P("cache"),
        ),
        out_specs=P("cache", "mp"),
        check_vma=False,
    )
```
